32 devices in a mesh: expert: 8 (over z, y), dp: 4 (over x, core).
Axes of the slice: x: 2, y: 2, z: 4, core: 2. Of those that a mesh axis runs over, the one named last changes fastest.
Arguments:
- out_grad: bfloat16 [2, 2048, 1024], P(None, ('expert', 'dp')), may hold values from -6 to 6
- sub_inputs: bfloat16 [2, 2048, 1024], P(None, ('expert', 'dp')), may hold values from -6 to 6
- route: int32 [2, 2048, 4, 1], P(None, ('expert', 'dp')), may hold values from 0 to 7; in each aligned block of 256 rows (0 to 255, 256 to 511, ..., all dimensions but the last counted through in order) at most 64 rows name the same one
- gate_scale: float32 [2, 2048, 4], P(None, ('expert', 'dp')), may hold values from 0.2 to 1
- merge_weight: bfloat16 [1024, 1024], P('expert'), may hold values from -0.1875 to 0.1875
- split_weight: bfloat16 [1024, 1024], P('expert'), may hold values from -0.1875 to 0.1875
- expert_gate: bfloat16 [8, 256, 768], P('expert'), may hold values from -0.375 to 0.375
- expert_up: bfloat16 [8, 256, 768], P('expert'), may hold values from -0.375 to 0.375
- expert_down: bfloat16 [8, 768, 256], P('expert'), may hold values from -0.21875 to 0.21875
Outputs:
- d_tokens: bfloat16 [2, 2048, 1024], P(None, ('expert', 'dp'))
- grad_gate: float32 [8, 256, 768], P('expert', 'dp')
- grad_up: float32 [8, 256, 768], P('expert', 'dp')
- grad_down: float32 [8, 768, 256], P('expert', 'dp')
The draws below stay inside these ranges and needn't reach their ends.
Inputs may be any that keep to these rules, and one draw needn't show every extreme that they name: `route`: in each micro-batch the 4 sub-tokens of one device's aligned block of 64 tokens name any one expert at most 64 times, and in some blocks exactly 64 times.
All inputs are finite; a program needn't handle non-finite values.
Results may differ from the reference program's by a relative error of at most 0.015.
Values may be sent and summed in bfloat16 or wider, within the bound.
No kernel may reach another device: no remote copies, remote signals or barrier semaphores. Data moves between devices by JAX's collectives and lax.ppermute only.
A program may use at most 64 MiB of HBM per device.

```python
import math
import jax
import jax.numpy as jnp
import numpy as np
from jax import lax

H = 4
S = 256
D = 1024
FFE = 768
MB = 2
TOK_DEV = 64
EXPERTS = 8
CAP = 64
TOKENS = 2048


def levels(key, dims, split, least, largest):
    gain, own = 1.0, jax.random.fold_in(key, 6)
    for position, parts in split:
        draws = jnp.exp(jax.random.uniform(jax.random.fold_in(own, position), (parts,), jnp.float32, least / len(split), largest / len(split)))
        gain = gain * jnp.repeat(draws, dims[position] // parts).reshape([-1 if axis == position else 1 for axis in range(len(dims))])
    return gain


def routed_block(own_key, own, number, rows, number_of, top, limit, skew):
    order = jax.random.permutation(own_key, number_of)
    heavy_load, ordinary = shares(number_of, rows * top, limit, skew, True), shares(number_of, rows * top, limit, skew, False)
    places = jnp.arange(number_of)

    def named(sizes, turn):
        used = int((sizes > 0).sum())
        fixed = max(1, used // 4)
        passed = fixed + (places - fixed + turn * (used - fixed)) % max(1, number_of - fixed)
        return jnp.zeros((number_of,), jnp.int32).at[order[jnp.where(places < fixed, places, passed)]].set(jnp.asarray(sizes, jnp.int32))

    sizes = jnp.where(number % 4 == 0, named(heavy_load, number // 4), named(ordinary, number - number // 4 - 1))
    mixed = jax.random.permutation(jax.random.fold_in(own, 3), number_of)
    source_of, receiver = mixed[0:number_of // 2 * 2:2], mixed[1:number_of // 2 * 2:2]
    slack = jnp.minimum(sizes[source_of] - 1, limit - sizes[receiver]) // 2
    slack = jnp.where((source_of == order[0]) | (receiver == order[0]) | (sizes[receiver] == 0), 0, jnp.maximum(slack, 0))
    passed = jax.random.randint(jax.random.fold_in(own, 4), (number_of // 2,), 0, 1 << 20) % (slack + 1)
    sizes = sizes.at[source_of].add(-passed).at[receiver].add(passed)
    members = jnp.searchsorted(jnp.cumsum(sizes), jnp.arange(rows * top), side="right").astype(jnp.int32)
    listing = members.reshape(top, rows).T
    listing = listing[jax.random.permutation(jax.random.fold_in(own, 1), rows)]
    turn = jax.random.randint(jax.random.fold_in(own, 2), (rows, 1), 0, top)
    return jnp.take_along_axis(listing, (jnp.arange(top)[None, :] + turn) % top, axis=1)


def shares(number_of, total, limit, skew, full):
    weights = [(1 << 20) // math.isqrt(standing ** skew) + 1 for standing in range(1, number_of + 1)]
    largest = limit if full else min(limit, max(-(-total // number_of), total * weights[0] // sum(weights)))
    least = 1 if total - largest >= number_of - 1 else 0
    counts, surplus = [largest] + [least] * (number_of - 1), total - largest - least * (number_of - 1)
    while surplus > 0:
        candidates = [i for i in range(1, number_of) if counts[i] < largest] or [i for i in range(1, number_of) if counts[i] < limit]
        pool, budget = sum([weights[i] for i in candidates]), surplus
        for i in candidates:
            extra = min(limit - counts[i], max(1, budget * weights[i] // pool), surplus)
            counts[i] = counts[i] + extra
            surplus = surplus - extra
    return np.array(counts)


def gaussian(key, shape, width, most, shards=(), kind=jnp.bfloat16):
    values = width * jax.random.normal(key, shape, jnp.float32)
    if shards:
        values = values * levels(key, shape, shards, -0.22, 0.18)
    return jnp.clip(values, -most, most).astype(kind)


def setup_inputs(seed: int = 0) -> dict:
    seeds = jax.random.split(jax.random.key(seed), 10)
    out_grad = gaussian(seeds[0], (MB, TOKENS, D), 1.0, 6.0, ((1, 32),))
    sub_inputs = gaussian(seeds[1], (MB, TOKENS, D), 1.0, 6.0, ((1, 32),))
    route_keys = jax.random.split(jax.random.fold_in(seeds[2], 1), MB * TOKENS * H // (TOK_DEV * H))
    route_turns = jax.random.permutation(jax.random.fold_in(seeds[2], 3), MB * TOKENS * H // (TOK_DEV * H))
    route = jax.vmap(lambda own, number: routed_block(jax.random.fold_in(seeds[2], 2), own, number, TOK_DEV * H, EXPERTS, 1, CAP, 2))(route_keys, route_turns).reshape((MB, TOKENS, H, 1))
    gate_scale = jnp.clip(0.2 + 0.8 * jax.random.uniform(seeds[3], (MB, TOKENS, H), jnp.float32) ** levels(seeds[3], (MB, TOKENS, H), ((1, 32),), -0.2, 0.2), 0.2, 1.0)
    merge_weight = gaussian(seeds[4], (D, D), D ** -0.5, 0.1875, ((0, 8),))
    split_weight = gaussian(seeds[5], (D, D), D ** -0.5, 0.1875, ((0, 8),))
    expert_gate = gaussian(seeds[6], (EXPERTS, S, FFE), S ** -0.5, 0.375, ((0, 8),))
    expert_up = gaussian(seeds[7], (EXPERTS, S, FFE), S ** -0.5, 0.375, ((0, 8),))
    expert_down = gaussian(seeds[8], (EXPERTS, FFE, S), FFE ** -0.5, 0.21875, ((0, 8),))
    return {"out_grad": out_grad, "sub_inputs": sub_inputs, "route": route, "gate_scale": gate_scale, "merge_weight": merge_weight, "split_weight": split_weight, "expert_gate": expert_gate, "expert_up": expert_up, "expert_down": expert_down}


def transposed(left_rows, right_rows):
    return lax.dot_general(left_rows, right_rows, (((1,), (1,)), ((), ())), preferred_element_type=jnp.float32)


def leading(left_rows, right_rows):
    return lax.dot_general(left_rows, right_rows, (((0,), (0,)), ((), ())), preferred_element_type=jnp.float32)


def slot_numbers(expert_ids, expert_count):
    row_count = expert_ids.shape[0]
    onehot = (expert_ids[:, None] == jnp.arange(expert_count, dtype=jnp.int32)[None, :]).astype(jnp.bfloat16)
    earlier_mask = (jnp.arange(row_count)[:, None] > jnp.arange(row_count)[None, :]).astype(jnp.bfloat16)
    before = jnp.dot(earlier_mask, onehot, preferred_element_type=jnp.float32)
    return jnp.sum(before * onehot.astype(jnp.float32), axis=1).astype(jnp.int32)


def expert_backward(inputs, grad_rows, weight_gate, weight_up, weight_down):
    pre_gate = jnp.dot(inputs, weight_gate, preferred_element_type=jnp.float32)
    pre_up = jnp.dot(inputs, weight_up, preferred_element_type=jnp.float32)
    sigma = jax.nn.sigmoid(pre_gate)
    activation = pre_gate * sigma
    slope_value = sigma * (1.0 + pre_gate * (1.0 - sigma))
    hidden = (activation * pre_up).astype(jnp.bfloat16)
    d_hidden = transposed(grad_rows, weight_down)
    delta_gate = (d_hidden * pre_up * slope_value).astype(jnp.bfloat16)
    delta_up = (d_hidden * activation).astype(jnp.bfloat16)
    delta_input = (transposed(delta_gate, weight_gate) + transposed(delta_up, weight_up)).astype(jnp.bfloat16)
    return delta_input, leading(inputs, delta_gate), leading(inputs, delta_up), leading(hidden, grad_rows)


def reference(out_grad, sub_inputs, route, gate_scale, merge_weight, split_weight, expert_gate, expert_up, expert_down):
    merged = transposed(out_grad.reshape(-1, D), merge_weight).astype(jnp.bfloat16)
    grad_rows = (gate_scale.reshape(-1, 1) * merged.reshape(-1, S).astype(jnp.float32)).astype(jnp.bfloat16)
    input_rows = sub_inputs.reshape(-1, S)
    expert_ids = route.reshape(-1).astype(jnp.int32)
    blocks = expert_ids.reshape(-1, TOK_DEV * H)
    slots = jax.vmap(partial_slots)(blocks).reshape(-1)
    block_count = blocks.shape[0]
    span = block_count * CAP
    total = expert_ids.shape[0]
    block_of = jnp.arange(total, dtype=jnp.int32) // (TOK_DEV * H)
    local_slot = (block_of * CAP + slots).astype(jnp.int32)
    input_pad = jnp.concatenate([input_rows, jnp.zeros((1, S), input_rows.dtype)], axis=0)
    grad_pad = jnp.concatenate([grad_rows, jnp.zeros((1, S), grad_rows.dtype)], axis=0)

    def per_expert(carry, expert):
        target = jnp.where(expert_ids == expert, local_slot, span).astype(jnp.int32)
        owner = jnp.full((span,), total, jnp.int32).at[target].set(jnp.arange(total, dtype=jnp.int32), mode="drop")
        delta, grad_gate, grad_up, grad_down = expert_backward(input_pad[owner], grad_pad[owner], expert_gate[expert], expert_up[expert], expert_down[expert])
        carry = carry.at[owner].set(delta, mode="drop")
        return carry, (grad_gate, grad_up, grad_down)

    start_rows = jnp.zeros((total, S), input_rows.dtype)
    delta_rows, stacked = lax.scan(per_expert, start_rows, jnp.arange(EXPERTS, dtype=jnp.int32))
    d_sub = delta_rows.reshape(-1, D)
    d_tokens = transposed(d_sub, split_weight).astype(jnp.bfloat16).reshape(MB, -1, D)
    return d_tokens, stacked[0], stacked[1], stacked[2]


def partial_slots(expert_ids):
    return slot_numbers(expert_ids, EXPERTS)
```

```python
import jax
import jax.numpy as jnp
from jax import lax
from jax.experimental import pallas as pl
from jax.experimental.pallas import tpu as pltpu
from jax.sharding import PartitionSpec as P

LANES = 128
VMEM_BYTES = 40 * 1024 * 1024


def transposed(left_rows, right_rows):
    return lax.dot_general(
        left_rows, right_rows, (((1,), (1,)), ((), ())), preferred_element_type=jnp.float32
    )


def leading(left_rows, right_rows):
    return lax.dot_general(
        left_rows, right_rows, (((0,), (0,)), ((), ())), preferred_element_type=jnp.float32
    )


def plain(left_rows, right_rows):
    return jnp.dot(left_rows, right_rows, preferred_element_type=jnp.float32)


def power_of_two(number):
    return number & (number - 1) == 0


def swap(value, axis, offset):
    return lax.ppermute(
        value, axis, [(index, index ^ offset) for index in range(lax.axis_size(axis))]
    )


def params():
    return pltpu.CompilerParams(vmem_limit_bytes=VMEM_BYTES)


def cost(flops, moved):
    return pl.CostEstimate(flops=flops, bytes_accessed=moved, transcendentals=0)


def gather_blocks(block, axis):
    span = lax.axis_size(axis)
    offsets = [0]
    while span > 1:
        radix = 4 if span % 4 == 0 and axis == "expert" else 2
        span //= radix
        block = jnp.concatenate(
            [block] + [swap(block, axis, step * span) for step in range(1, radix)]
        )
        offsets = [old ^ (step * span) for step in range(radix) for old in offsets]
    return block, offsets


def route_kernel(batch_count, slots_per, key_count, ids_ref, rows_ref, send_ref, across_ref, down_ref):
    head_count, row_count = ids_ref.shape
    width = rows_ref.shape[1] // head_count
    lane = lax.broadcasted_iota(jnp.int32, (1, row_count), 1)
    batch = jnp.zeros((1, row_count), jnp.int32)
    for number in range(1, batch_count):
        batch = batch + (lane >= number * (row_count // batch_count)).astype(jnp.int32)
    keys = [ids_ref[head : head + 1, :] * batch_count + batch for head in range(head_count)]
    key = jnp.concatenate(keys, axis=1)
    total = head_count * row_count
    onehot = lax.broadcasted_iota(jnp.int32, (key_count, total), 0) == key
    earlier = lax.broadcasted_iota(jnp.int32, (total, total), 0) < lax.broadcasted_iota(
        jnp.int32, (total, total), 1
    )
    before = plain(
        onehot.astype(jnp.float32).astype(jnp.bfloat16),
        earlier.astype(jnp.float32).astype(jnp.bfloat16),
    )
    slot = jnp.sum(jnp.where(onehot, before, 0.0), axis=0, keepdims=True).astype(jnp.int32)
    target = key * slots_per + slot
    send_ref[...] = scatter_rows(
        target,
        [rows_ref[:, head * width : (head + 1) * width] for head in range(head_count)],
        send_ref.shape[0],
    )
    across = jnp.concatenate(
        [target[:, head * row_count : (head + 1) * row_count] for head in range(head_count)], axis=0
    )
    across_ref[...] = across
    down_ref[...] = across.astype(jnp.float32).T.astype(jnp.int32)


def scatter_rows(target, row_list, slot_count):
    total = target.shape[1]
    picked = lax.broadcasted_iota(jnp.int32, (slot_count, total), 0) == target
    return plain(
        picked.astype(jnp.float32).astype(jnp.bfloat16), jnp.concatenate(row_list, axis=0)
    ).astype(jnp.bfloat16)


def merge_kernel(offsets, block_rows, token_ref, weight_ref, *rest):
    out_refs, held = rest[:-1], rest[-1]
    here = lax.axis_index("expert")
    for place, offset in enumerate(offsets):
        start = pl.multiple_of((here ^ offset) * block_rows, block_rows)
        held[pl.ds(start, block_rows), :] = weight_ref[
            place * block_rows : (place + 1) * block_rows, :
        ]
    count = out_refs[0].shape[0]
    result = transposed(token_ref[...], held[...]).astype(jnp.bfloat16)
    for number, out_ref in enumerate(out_refs):
        out_ref[...] = result[number * count : (number + 1) * count]


def assemble(offsets, part_refs, width):
    here = lax.axis_index("dp")
    parts = [ref[...].astype(jnp.float32) for ref in part_refs]
    group = len(parts)
    rows, held = parts[0].shape
    lane = lax.broadcasted_iota(jnp.int32, (rows, LANES), 1)
    blocks = []
    for expert in range(held // width):
        base = expert * width // LANES * LANES
        inside = expert * width - base
        block = jnp.zeros((rows, LANES), jnp.float32)
        for offset, part in zip(offsets, parts):
            first = (here ^ offset) * width
            shift = lax.rem(first + LANES - inside, LANES)
            moved = pltpu.roll(part[:, base : base + LANES], shift, 1)
            block = jnp.where((lane >= first) & (lane < first + width), moved, block)
        blocks.append(block)
    return jnp.concatenate(blocks, axis=1)


def grad_kernel(offsets, width, scale_ref, across_ref, *rest):
    part_refs, send_ref = rest[:-1], rest[-1]
    merged = (
        part_refs[0][...].astype(jnp.float32)
        if offsets is None
        else assemble(offsets, part_refs, width)
    )
    head_count = across_ref.shape[0]
    sub_width = merged.shape[1] // head_count
    rows = [
        (
            scale_ref[:, head : head + 1] * merged[:, head * sub_width : (head + 1) * sub_width]
        ).astype(jnp.bfloat16)
        for head in range(head_count)
    ]
    target = jnp.concatenate([across_ref[head : head + 1, :] for head in range(head_count)], axis=1)
    send_ref[...] = scatter_rows(target, rows, send_ref.shape[0])


def delta_kernel(input_ref, grad_ref, gate_ref, up_ref, down_ref, delta_ref, both_ref, hidden_ref):
    inputs = input_ref[...]
    hidden_width = gate_ref.shape[1]
    pre_gate = plain(inputs, gate_ref[...])
    pre_up = plain(inputs, up_ref[...])
    d_hidden = transposed(grad_ref[...], down_ref[...])
    sigma = jax.nn.sigmoid(pre_gate)
    activation = pre_gate * sigma
    slope_value = sigma * (1.0 + pre_gate * (1.0 - sigma))
    hidden_ref[...] = (activation * pre_up).astype(jnp.bfloat16)
    delta_gate = (d_hidden * pre_up * slope_value).astype(jnp.bfloat16)
    delta_up = (d_hidden * activation).astype(jnp.bfloat16)
    both_ref[:, :hidden_width] = delta_gate
    both_ref[:, hidden_width:] = delta_up
    delta_ref[...] = (
        transposed(delta_gate, gate_ref[...]) + transposed(delta_up, up_ref[...])
    ).astype(jnp.bfloat16)


def weight_kernel(
    group, input_ref, grad_ref, both_ref, hidden_ref, keep_a, keep_b, send_a, send_b, held_a, held_b
):
    here = lax.axis_index("dp")
    held_a[...] = leading(input_ref[...], both_ref[...])
    held_b[...] = leading(hidden_ref[...], grad_ref[...])
    for held, keep, send in ((held_a, keep_a, send_a), (held_b, keep_b, send_b)):
        rows = held.shape[0] // group
        for place in range(group // 2):
            own = pl.multiple_of((here ^ (2 * place)) * rows, rows)
            keep[place] = held[pl.ds(own, rows), :]
            other = pl.multiple_of((here ^ (2 * place + 1)) * rows, rows)
            send[place] = held[pl.ds(other, rows), :].astype(jnp.bfloat16)


def halve_kernel(keep_a, keep_b, got_a, got_b, next_a, next_b, send_a, send_b):
    for keep, got, own, send in (
        (keep_a, got_a, next_a, send_a),
        (keep_b, got_b, next_b, send_b),
    ):
        count = own.shape[0]
        for place in range(count):
            own[place] = keep[2 * place] + got[2 * place].astype(jnp.float32)
            send[place] = (keep[2 * place + 1] + got[2 * place + 1].astype(jnp.float32)).astype(
                jnp.bfloat16
            )


def last_kernel(keep_a, keep_b, got_a, got_b, gate_ref, up_ref, down_ref):
    width = gate_ref.shape[2]
    summed = keep_a[0] + got_a[0].astype(jnp.float32)
    gate_ref[0] = summed[:, :width]
    up_ref[0] = summed[:, width:]
    down_ref[0] = keep_b[0] + got_b[0].astype(jnp.float32)


def order_kernel(dp_offsets, offsets, block_rows, weight_ref, out_ref):
    here, group = lax.axis_index("expert"), lax.axis_index("dp")
    place = 0
    for dp_offset in dp_offsets:
        for offset in offsets:
            start = ((here ^ offset) * len(dp_offsets) + (group ^ dp_offset)) * block_rows
            out_ref[pl.ds(pl.multiple_of(start, block_rows), block_rows), :] = weight_ref[
                place * block_rows : (place + 1) * block_rows, :
            ]
            place += 1


def split_kernel(down_ref, back_ref, weight_ref, out_ref):
    row_count, head_count = down_ref.shape
    slot_count, width = back_ref.shape
    lane = lax.broadcasted_iota(jnp.int32, (row_count, slot_count), 1)
    picked = jnp.concatenate(
        [
            (lane == down_ref[:, head : head + 1]).astype(jnp.float32).astype(jnp.bfloat16)
            for head in range(head_count)
        ],
        axis=0,
    )
    rows = plain(picked, back_ref[...]).astype(jnp.bfloat16)
    d_sub = jnp.concatenate(
        [rows[head * row_count : (head + 1) * row_count] for head in range(head_count)], axis=1
    )
    out_ref[...] = transposed(d_sub, weight_ref[...]).astype(jnp.bfloat16)


def on_device(
    out_grad,
    sub_inputs,
    route,
    gate_scale,
    merge_weight,
    split_weight,
    expert_gate,
    expert_up,
    expert_down,
):
    batch_count, tok_count, model_width = out_grad.shape
    head_count = route.shape[2]
    sub_width = model_width // head_count
    expert_count = lax.axis_size("expert")
    group = lax.axis_size("dp")
    here = lax.axis_index("dp")
    slots_per = 2 * tok_count * head_count // expert_count
    row_count = batch_count * tok_count
    key_count = expert_count * batch_count
    slot_count = key_count * slots_per
    shard_rows = merge_weight.shape[0]
    hidden_width = expert_gate.shape[2]
    bf16, f32 = jnp.bfloat16, jnp.float32
    block_rows = shard_rows // group
    in_blocks = (
        shard_rows == LANES
        and block_rows % 16 == 0
        and power_of_two(expert_count)
        and power_of_two(group)
    )
    shape = jax.ShapeDtypeStruct
    tokens = out_grad.reshape(row_count, model_width)
    rows_in = sub_inputs.reshape(row_count, model_width)
    scale = gate_scale.reshape(row_count, head_count)
    ids = route.reshape(row_count, head_count).T

    if in_blocks:
        merge_block = lax.dynamic_slice_in_dim(merge_weight, here * block_rows, block_rows, 0)
        split_block = lax.dynamic_slice_in_dim(split_weight, here * block_rows, block_rows, 0)
        merge_part, offsets = gather_blocks(merge_block, "expert")
        tokens_all, dp_offsets = gather_blocks(tokens, "dp")
    else:
        whole_merge = lax.all_gather(merge_weight, "expert", axis=0, tiled=True)
        whole_split = lax.all_gather(split_weight, "expert", axis=0, tiled=True)

    def route_body(*refs):
        route_kernel(batch_count, slots_per, key_count, *refs)

    send_inputs, across, down = pl.pallas_call(
        route_body,
        out_shape=(
            shape((slot_count, sub_width), bf16),
            shape((head_count, row_count), jnp.int32),
            shape((row_count, head_count), jnp.int32),
        ),
        compiler_params=params(),
        cost_estimate=cost(2 * slot_count * row_count * model_width, 2 * slot_count * sub_width),
    )(ids, rows_in)

    def exchange(rows):
        return lax.all_to_all(
            rows.reshape(expert_count, -1, sub_width), "expert", 0, 0, tiled=True
        ).reshape(slot_count, sub_width)

    recv_inputs = exchange(send_inputs)

    if in_blocks:

        def merge_body(*refs):
            merge_kernel(offsets, block_rows, *refs)

        part_width = expert_count * block_rows
        parts = pl.pallas_call(
            merge_body,
            out_shape=tuple(shape((row_count, part_width), bf16) for _ in range(group)),
            scratch_shapes=[pltpu.VMEM((part_width, model_width), bf16)],
            compiler_params=params(),
            cost_estimate=cost(
                2 * group * row_count * part_width * model_width, 2 * group * row_count * model_width
            ),
        )(tokens_all, merge_part)
        parts = [
            part if offset == 0 else swap(part, "dp", offset)
            for part, offset in zip(parts, dp_offsets)
        ]
    else:
        dp_offsets = None
        parts = [transposed(tokens, whole_merge).astype(bf16)]

    def grad_body(*refs):
        grad_kernel(dp_offsets, block_rows, *refs)

    send_grads = pl.pallas_call(
        grad_body,
        out_shape=shape((slot_count, sub_width), bf16),
        compiler_params=params(),
        cost_estimate=cost(2 * slot_count * row_count * model_width, 2 * slot_count * sub_width),
    )(scale, across, *parts)
    recv_grads = exchange(send_grads)

    weight_gate = expert_gate[0]
    weight_up = expert_up[0]
    weight_down = expert_down[0]
    steps = 4
    chunk = slot_count // steps
    by_rows = lambda width: pl.BlockSpec((chunk, width), lambda step: (step, 0))
    held = lambda array: pl.BlockSpec(array.shape, lambda step: (0, 0))
    delta, both, hidden = pl.pallas_call(
        delta_kernel,
        grid=(steps,),
        in_specs=[
            by_rows(sub_width),
            by_rows(sub_width),
            held(weight_gate),
            held(weight_up),
            held(weight_down),
        ],
        out_specs=(by_rows(sub_width), by_rows(2 * hidden_width), by_rows(hidden_width)),
        out_shape=(
            shape((slot_count, sub_width), bf16),
            shape((slot_count, 2 * hidden_width), bf16),
            shape((slot_count, hidden_width), bf16),
        ),
        compiler_params=params(),
        cost_estimate=cost(10 * slot_count * sub_width * hidden_width, 8 * slot_count * hidden_width),
    )(recv_inputs, recv_grads, weight_gate, weight_up, weight_down)
    returned = exchange(delta)

    half = group // 2
    gate_rows, down_rows = sub_width // group, hidden_width // group

    def weight_body(*refs):
        weight_kernel(group, *refs)

    keep_a, keep_b, send_a, send_b = pl.pallas_call(
        weight_body,
        out_shape=(
            shape((half, gate_rows, 2 * hidden_width), f32),
            shape((half, down_rows, sub_width), f32),
            shape((half, gate_rows, 2 * hidden_width), bf16),
            shape((half, down_rows, sub_width), bf16),
        ),
        scratch_shapes=[
            pltpu.VMEM((sub_width, 2 * hidden_width), f32),
            pltpu.VMEM((hidden_width, sub_width), f32),
        ],
        compiler_params=params(),
        cost_estimate=cost(6 * slot_count * sub_width * hidden_width, 8 * slot_count * hidden_width),
    )(recv_inputs, recv_grads, both, hidden)
    offset = 1
    while 2 * offset < group:
        half //= 2
        got_a, got_b = swap(send_a, "dp", offset), swap(send_b, "dp", offset)
        keep_a, keep_b, send_a, send_b = pl.pallas_call(
            halve_kernel,
            out_shape=(
                shape((half, gate_rows, 2 * hidden_width), f32),
                shape((half, down_rows, sub_width), f32),
                shape((half, gate_rows, 2 * hidden_width), bf16),
                shape((half, down_rows, sub_width), bf16),
            ),
            compiler_params=params(),
        )(keep_a, keep_b, got_a, got_b)
        offset *= 2
    got_a, got_b = swap(send_a, "dp", offset), swap(send_b, "dp", offset)
    shared_gate, shared_up, shared_down = pl.pallas_call(
        last_kernel,
        out_shape=(
            shape((1, gate_rows, hidden_width), f32),
            shape((1, gate_rows, hidden_width), f32),
            shape((1, down_rows, sub_width), f32),
        ),
        compiler_params=params(),
    )(keep_a, keep_b, got_a, got_b)

    if in_blocks:
        split_part, _ = gather_blocks(split_block, "expert")
        split_all, _ = gather_blocks(split_part, "dp")

        def order_body(*refs):
            order_kernel(dp_offsets, offsets, block_rows, *refs)

        whole_split = pl.pallas_call(
            order_body,
            out_shape=shape((model_width, model_width), bf16),
            compiler_params=params(),
        )(split_all)
    d_tokens = pl.pallas_call(
        split_kernel,
        out_shape=shape((row_count, model_width), bf16),
        compiler_params=params(),
    )(down, returned, whole_split).reshape(batch_count, tok_count, model_width)
    return (d_tokens, shared_gate, shared_up, shared_down)


def solution(mesh):
    placed = (
        P(None, ("expert", "dp"), None),
        P(None, ("expert", "dp"), None),
        P(None, ("expert", "dp"), None, None),
        P(None, ("expert", "dp"), None),
        P("expert", None),
        P("expert", None),
        P("expert", None, None),
        P("expert", None, None),
        P("expert", None, None),
    )
    return jax.shard_map(
        on_device,
        mesh=mesh,
        in_specs=placed,
        out_specs=(
            P(None, ("expert", "dp"), None),
            P("expert", "dp", None),
            P("expert", "dp", None),
            P("expert", "dp", None),
        ),
        check_vma=False,
    )
```

```python
import jax
import jax.numpy as jnp
from jax import lax
from jax.experimental import pallas as pl
from jax.experimental.pallas import tpu as pltpu
from jax.sharding import PartitionSpec as P

LANES = 128
MERGE_COST = 5000000000
VMEM_BYTES = 16 * 1024 * 1024


def transposed(left_rows, right_rows):
    return lax.dot_general(
        left_rows, right_rows, (((1,), (1,)), ((), ())), preferred_element_type=jnp.float32
    )


def leading(left_rows, right_rows):
    return lax.dot_general(
        left_rows, right_rows, (((0,), (0,)), ((), ())), preferred_element_type=jnp.float32
    )


def plain(left_rows, right_rows):
    return jnp.dot(left_rows, right_rows, preferred_element_type=jnp.float32)


def power_of_two(number):
    return number & (number - 1) == 0


def swap(value, axis, offset):
    return lax.ppermute(
        value, axis, [(index, index ^ offset) for index in range(lax.axis_size(axis))]
    )


def params():
    return pltpu.CompilerParams(vmem_limit_bytes=VMEM_BYTES)


def in_hbm(*arrays):
    return [pltpu.with_memory_space_constraint(array, pltpu.HBM) for array in arrays]


def in_vmem(*arrays):
    return [pltpu.with_memory_space_constraint(array, pltpu.VMEM) for array in arrays]


def after(value, *earlier):
    return lax.optimization_barrier((value, *earlier))[0]


def cost(flops, moved):
    return pl.CostEstimate(flops=flops, bytes_accessed=moved, transcendentals=0)


def gather_blocks(block, axis, *gate):
    span = lax.axis_size(axis)
    blocks, offsets = [block], [0]
    while span > 1:
        radix = 4 if span % 4 == 0 else 2
        span //= radix
        block = jnp.concatenate(blocks) if len(blocks) > 1 else blocks[0]
        if span == 1 and gate:
            block = after(block, *gate)
        steps = [step * span for step in range(1, radix)]
        blocks = [block] + [swap(block, axis, step) for step in steps]
        offsets = offsets + [old ^ step for step in steps for old in offsets]
    return blocks, offsets


def gather_parts(block, axis):
    span = lax.axis_size(axis)
    blocks, offsets = [block], [0]
    while span > 1:
        span //= 2
        blocks = blocks + [swap(old, axis, span) for old in blocks]
        offsets = offsets + [old ^ span for old in offsets]
    return blocks, offsets


def place_rows(offsets, count, block_refs, out_ref):
    here = lax.axis_index("expert")
    held = [(ref, row) for ref in block_refs for row in range(0, ref.shape[0], count)]
    for offset, (ref, row) in zip(offsets, held):
        start = pl.multiple_of((here ^ offset) * count, count)
        out_ref[pl.ds(start, count), :] = ref[row : row + count, :]


def route_kernel(
    batch_count, slots_per, key_count, ids_ref, rows_ref, weight_refs, send_ref, across_ref, down_ref, block_refs, sems
):
    here = lax.axis_index("dp")
    copies = []
    for number, (weight_ref, block_ref) in enumerate(zip(weight_refs, block_refs)):
        count = block_ref.shape[0]
        own = weight_ref.at[pl.ds(pl.multiple_of(here * count, count), count), :]
        copies.append(pltpu.make_async_copy(own, block_ref, sems.at[number]))
        copies[-1].start()
    head_count, row_count = ids_ref.shape
    width = rows_ref.shape[1] // head_count
    lane = lax.broadcasted_iota(jnp.int32, (1, row_count), 1)
    batch = jnp.zeros((1, row_count), jnp.int32)
    for number in range(1, batch_count):
        batch = batch + (lane >= number * (row_count // batch_count)).astype(jnp.int32)
    keys = [ids_ref[head : head + 1, :] * batch_count + batch for head in range(head_count)]
    key = jnp.concatenate(keys, axis=1)
    total = head_count * row_count
    onehot = lax.broadcasted_iota(jnp.int32, (key_count, total), 0) == key
    earlier = lax.broadcasted_iota(jnp.int32, (total, total), 0) < lax.broadcasted_iota(
        jnp.int32, (total, total), 1
    )
    before = plain(
        onehot.astype(jnp.float32).astype(jnp.bfloat16),
        earlier.astype(jnp.float32).astype(jnp.bfloat16),
    )
    slot = jnp.sum(jnp.where(onehot, before, 0.0), axis=0, keepdims=True).astype(jnp.int32)
    target = key * slots_per + slot
    send_ref[...] = scatter_rows(
        target,
        [rows_ref[:, head * width : (head + 1) * width] for head in range(head_count)],
        send_ref.shape[0],
    )
    across = jnp.concatenate(
        [target[:, head * row_count : (head + 1) * row_count] for head in range(head_count)], axis=0
    )
    across_ref[...] = across
    down_ref[...] = across.astype(jnp.float32).T.astype(jnp.int32)
    for copy in copies:
        copy.wait()


def scatter_rows(target, row_list, slot_count):
    total = target.shape[1]
    picked = lax.broadcasted_iota(jnp.int32, (slot_count, total), 0) == target
    return plain(
        picked.astype(jnp.float32).astype(jnp.bfloat16), jnp.concatenate(row_list, axis=0)
    ).astype(jnp.bfloat16)


def merge_kernel(offsets, count, token_refs, weight_refs, out_refs, held):
    place_rows(offsets, count, weight_refs, held)
    for token_ref, out_ref in zip(token_refs, out_refs):
        out_ref[...] = transposed(token_ref[...], held[...]).astype(jnp.bfloat16)


def assemble(offsets, part_refs, width):
    here = lax.axis_index("dp")
    parts = [ref[...].astype(jnp.float32) for ref in part_refs]
    group = len(parts)
    rows, held = parts[0].shape
    lane = lax.broadcasted_iota(jnp.int32, (rows, LANES), 1)
    blocks = []
    for expert in range(held // width):
        base = expert * width // LANES * LANES
        inside = expert * width - base
        block = jnp.zeros((rows, LANES), jnp.float32)
        for offset, part in zip(offsets, parts):
            first = (here ^ offset) * width
            shift = lax.rem(first + LANES - inside, LANES)
            moved = pltpu.roll(part[:, base : base + LANES], shift, 1)
            block = jnp.where((lane >= first) & (lane < first + width), moved, block)
        blocks.append(block)
    return jnp.concatenate(blocks, axis=1)


def grad_kernel(offsets, width, scale_ref, across_ref, *rest):
    part_refs, send_ref = rest[:-1], rest[-1]
    merged = (
        part_refs[0][...].astype(jnp.float32)
        if offsets is None
        else assemble(offsets, part_refs, width)
    )
    head_count = across_ref.shape[0]
    sub_width = merged.shape[1] // head_count
    rows = [
        (
            scale_ref[:, head : head + 1] * merged[:, head * sub_width : (head + 1) * sub_width]
        ).astype(jnp.bfloat16)
        for head in range(head_count)
    ]
    target = jnp.concatenate([across_ref[head : head + 1, :] for head in range(head_count)], axis=1)
    send_ref[...] = scatter_rows(target, rows, send_ref.shape[0])


def chunks(count, chunk):
    return [slice(start, start + chunk) for start in range(0, count, chunk)]


def fetch(source_ref, held_ref, sems, rows):
    copies = [
        pltpu.make_async_copy(source_ref.at[part, :], held_ref.at[part, :], sems.at[number])
        for number, part in enumerate(rows)
    ]
    for copy in copies:
        copy.start()
    return copies


def send_out(source_ref, target_ref, part, sem):
    copy = pltpu.make_async_copy(source_ref.at[part, :], target_ref.at[part, :], sem)
    copy.start()
    return copy


def forward_kernel(
    rows, input_ref, gate_ref, up_ref, inputs_out, hidden_out, slope_out, activation_out,
    inputs_held, gate_held, up_held, hidden, slope, activation_held, sems, weight_sems, out_sems
):
    copies = fetch(input_ref, inputs_held, sems, rows)
    weights = [
        pltpu.make_async_copy(gate_ref, gate_held, weight_sems.at[0]),
        pltpu.make_async_copy(up_ref, up_held, weight_sems.at[1]),
    ]
    for copy in weights:
        copy.start()
    for copy in weights:
        copy.wait()
    outs = []
    for number, (part, copy) in enumerate(zip(rows, copies)):
        copy.wait()
        inputs = inputs_held[part, :]
        pre_gate = plain(inputs, gate_held[...])
        pre_up = plain(inputs, up_held[...])
        sigma = jax.nn.sigmoid(pre_gate)
        activation = pre_gate * sigma
        slope_value = sigma * (1.0 + pre_gate * (1.0 - sigma))
        hidden[part, :] = (activation * pre_up).astype(jnp.bfloat16)
        slope[part, :] = (pre_up * slope_value).astype(jnp.bfloat16)
        activation_held[part, :] = activation.astype(jnp.bfloat16)
        for place, (source, target) in enumerate(
            (
                (inputs_held, inputs_out),
                (hidden, hidden_out),
                (slope, slope_out),
                (activation_held, activation_out),
            )
        ):
            outs.append(send_out(source, target, part, out_sems.at[place, number]))
    for copy in outs:
        copy.wait()


def delta_kernel(
    rows, grad_ref, slope_ref, activation_ref, gate_ref, up_ref, down_ref,
    both_ref, delta_ref, grads_out,
    slope, activation, gate_held, up_held, down_held, out, sems, weight_sems, out_sems
):
    hidden_width = gate_ref.shape[1]
    weights = [
        pltpu.make_async_copy(source, target, weight_sems.at[number])
        for number, (source, target) in enumerate(
            ((down_ref, down_held), (gate_ref, gate_held), (up_ref, up_held))
        )
    ]
    copies = []
    weights[0].start()
    for number, part in enumerate(rows):
        copies.append(
            [
                send_out(source, target, part, sems.at[place, number])
                for place, (source, target) in enumerate(
                    ((slope_ref, slope), (activation_ref, activation))
                )
            ]
        )
        if number == 0:
            weights[1].start()
            weights[2].start()
    weights[0].wait()
    outs = []
    for number, (part, arrived) in enumerate(zip(rows, copies)):
        d_hidden = transposed(grad_ref[part, :], down_held[...])
        arrived[0].wait()
        arrived[1].wait()
        delta_gate = (d_hidden * slope[part, :].astype(jnp.float32)).astype(jnp.bfloat16)
        delta_up = (d_hidden * activation[part, :].astype(jnp.float32)).astype(jnp.bfloat16)
        both_ref[part, :hidden_width] = delta_gate
        both_ref[part, hidden_width:] = delta_up
        if number == 0:
            weights[1].wait()
            weights[2].wait()
        out[part, :] = (
            transposed(delta_gate, gate_held[...]) + transposed(delta_up, up_held[...])
        ).astype(jnp.bfloat16)
        outs.append(send_out(out, delta_ref, part, out_sems.at[0, number]))
        outs.append(send_out(grad_ref, grads_out, part, out_sems.at[1, number]))
    for copy in outs:
        copy.wait()


def weight_kernel(
    group, input_ref, grad_ref, both_ref, hidden_ref, keep_a, keep_b, send_a, send_b,
    inputs_held, grads_held, hidden_held, held_a, held_b, sems
):
    here = lax.axis_index("dp")
    copies = [
        pltpu.make_async_copy(source, target, sems.at[number])
        for number, (source, target) in enumerate(
            ((input_ref, inputs_held), (grad_ref, grads_held), (hidden_ref, hidden_held))
        )
    ]
    for copy in copies:
        copy.start()
    copies[0].wait()
    held_a[...] = leading(inputs_held[...], both_ref[...])
    copies[1].wait()
    copies[2].wait()
    held_b[...] = leading(hidden_held[...], grads_held[...])
    give_weights(group, here, held_a, held_b, keep_a, keep_b, send_a, send_b)


def give_weights(group, here, held_a, held_b, keep_a, keep_b, send_a, send_b):
    for held, keep, send in ((held_a, keep_a, send_a), (held_b, keep_b, send_b)):
        rows = held.shape[0] // group
        for place in range(group // 2):
            own = pl.multiple_of((here ^ (2 * place)) * rows, rows)
            keep[place] = held[pl.ds(own, rows), :]
            other = pl.multiple_of((here ^ (2 * place + 1)) * rows, rows)
            send[place] = held[pl.ds(other, rows), :].astype(jnp.bfloat16)


def halve_kernel(keep_a, keep_b, got_a, got_b, next_a, next_b, send_a, send_b):
    for keep, got, own, send in (
        (keep_a, got_a, next_a, send_a),
        (keep_b, got_b, next_b, send_b),
    ):
        count = own.shape[0]
        for place in range(count):
            own[place] = keep[2 * place] + got[2 * place].astype(jnp.float32)
            send[place] = (keep[2 * place + 1] + got[2 * place + 1].astype(jnp.float32)).astype(
                jnp.bfloat16
            )


def last_kernel(keep_a, keep_b, got_a, got_b, gate_ref, up_ref, down_ref):
    width = gate_ref.shape[2]
    summed = keep_a[0] + got_a[0].astype(jnp.float32)
    gate_ref[0] = summed[:, :width]
    up_ref[0] = summed[:, width:]
    down_ref[0] = keep_b[0] + got_b[0].astype(jnp.float32)


def interleave_kernel(offsets, count, part_refs, out_ref):
    here = lax.axis_index("dp")
    for offset, part_ref in zip(offsets, part_refs):
        for place in range(part_ref.shape[0] // count):
            start = (place * len(offsets) + (here ^ offset)) * count
            out_ref[pl.ds(pl.multiple_of(start, count), count), :] = part_ref[
                place * count : (place + 1) * count, :
            ]


def split_kernel(down_ref, back_ref, weight_ref, out_ref, back, held, sems):
    row_count, head_count = down_ref.shape
    slot_count, width = back_ref.shape
    (copy,) = fetch(back_ref, back, sems, [slice(0, slot_count)])
    lane = lax.broadcasted_iota(jnp.int32, (row_count, slot_count), 1)
    picked = jnp.concatenate(
        [
            (lane == down_ref[:, head : head + 1]).astype(jnp.float32).astype(jnp.bfloat16)
            for head in range(head_count)
        ],
        axis=0,
    )
    copy.wait()
    rows = plain(picked, back[...]).astype(jnp.bfloat16)
    for head in range(head_count):
        held[:, head * width : (head + 1) * width] = rows[head * row_count : (head + 1) * row_count]
    out_ref[...] = transposed(held[...], weight_ref[...]).astype(jnp.bfloat16)


def on_device(
    out_grad,
    sub_inputs,
    route,
    gate_scale,
    merge_weight,
    split_weight,
    expert_gate,
    expert_up,
    expert_down,
):
    batch_count, tok_count, model_width = out_grad.shape
    head_count = route.shape[2]
    sub_width = model_width // head_count
    expert_count = lax.axis_size("expert")
    group = lax.axis_size("dp")
    here = lax.axis_index("dp")
    slots_per = 2 * tok_count * head_count // expert_count
    row_count = batch_count * tok_count
    key_count = expert_count * batch_count
    slot_count = key_count * slots_per
    shard_rows = merge_weight.shape[0]
    hidden_width = expert_gate.shape[2]
    bf16, f32 = jnp.bfloat16, jnp.float32
    block_rows = shard_rows // group
    in_blocks = (
        shard_rows == LANES
        and block_rows % 16 == 0
        and power_of_two(expert_count)
        and power_of_two(group)
    )
    shape = jax.ShapeDtypeStruct
    tokens = out_grad.reshape(row_count, model_width)
    rows_in = sub_inputs.reshape(row_count, model_width)
    scale = gate_scale.reshape(row_count, head_count)
    ids = route.reshape(row_count, head_count).T

    if in_blocks:
        merge_block = lax.dynamic_slice_in_dim(merge_weight, here * block_rows, block_rows, 0)
        merge_blocks, offsets = gather_blocks(merge_block, "expert")

    def route_body(*refs):
        count = 1 if in_blocks else 0
        route_kernel(
            batch_count,
            slots_per,
            key_count,
            refs[0],
            refs[1],
            refs[2 : 2 + count],
            *refs[2 + count : 5 + count],
            refs[5 + count : -1],
            refs[-1],
        )

    block_shape = shape((block_rows, model_width), bf16)
    send_inputs, across, down, *blocks = pl.pallas_call(
        route_body,
        out_shape=(
            shape((slot_count, sub_width), bf16),
            shape((head_count, row_count), jnp.int32),
            shape((row_count, head_count), jnp.int32),
        )
        + ((block_shape,) if in_blocks else ()),
        in_specs=[pl.BlockSpec(memory_space=pltpu.VMEM)] * 2
        + [pl.BlockSpec(memory_space=pl.ANY)] * (1 if in_blocks else 0),
        scratch_shapes=[pltpu.SemaphoreType.DMA((1,))],
        compiler_params=params(),
        cost_estimate=cost(2 * slot_count * row_count * model_width, 2 * slot_count * sub_width),
    )(ids, *in_hbm(rows_in), *(in_hbm(split_weight) if in_blocks else ()))

    if in_blocks:
        split_joined = gather_blocks(after(blocks[0], merge_blocks[0]), "expert")[0]
        token_parts, dp_offsets = gather_parts(after(tokens, send_inputs), "dp")
        send_inputs = after(send_inputs, split_joined[0])
    else:
        whole_merge = lax.all_gather(merge_weight, "expert", axis=0, tiled=True)
        whole_split = lax.all_gather(split_weight, "expert", axis=0, tiled=True)

    def exchange(rows):
        return lax.all_to_all(
            rows.reshape(expert_count, -1, sub_width), "expert", 0, 0, tiled=True
        ).reshape(slot_count, sub_width)

    recv_inputs = exchange(send_inputs)

    if in_blocks:

        def merge_body(*refs):
            last = group + len(merge_blocks)
            merge_kernel(
                offsets, block_rows, refs[:group], refs[group:last], refs[last:-1], refs[-1]
            )

        part_width = expert_count * block_rows
        parts = pl.pallas_call(
            merge_body,
            out_shape=tuple(shape((row_count, part_width), bf16) for _ in range(group)),
            scratch_shapes=[pltpu.VMEM((part_width, model_width), bf16)],
            compiler_params=params(),
            cost_estimate=cost(MERGE_COST, 1),
        )(*token_parts, *merge_blocks)
        parts = [
            part if offset == 0 else swap(part, "dp", offset)
            for part, offset in zip(parts, dp_offsets)
        ]
    else:
        dp_offsets = None
        parts = [transposed(tokens, whole_merge).astype(bf16)]

    def grad_body(*refs):
        grad_kernel(dp_offsets, block_rows, *refs)

    send_grads = pl.pallas_call(
        grad_body,
        out_shape=shape((slot_count, sub_width), bf16),
        compiler_params=params(),
        cost_estimate=cost(2 * slot_count * row_count * model_width, 2 * slot_count * sub_width),
    )(scale, across, *parts)
    weight_gate = expert_gate[0]
    weight_up = expert_up[0]
    weight_down = expert_down[0]
    rows = chunks(slot_count, slot_count // 4)
    anywhere = pl.BlockSpec(memory_space=pl.ANY)
    inside = pl.BlockSpec(memory_space=pltpu.VMEM)
    wide = pltpu.VMEM((slot_count, hidden_width), bf16)
    narrow = pltpu.VMEM((slot_count, sub_width), bf16)
    upright = pltpu.VMEM(weight_gate.shape, bf16)
    lying = pltpu.VMEM(weight_down.shape, bf16)
    sems = lambda *dims: pltpu.SemaphoreType.DMA(dims)
    steps = len(rows)
    wide_out = pltpu.HBM((slot_count, hidden_width), bf16)
    narrow_out = pltpu.HBM((slot_count, sub_width), bf16)

    if in_blocks:
        split_far = swap(after(split_joined[0], parts[-1]), "expert", 1)
        recv_grads = exchange(after(send_grads, recv_inputs, split_far))

        def order_body(*refs):
            place_rows(offsets, block_rows, refs[:-1], refs[-1])

        column = pl.pallas_call(
            order_body,
            out_shape=shape((part_width, model_width), bf16),
            compiler_params=params(),
        )(split_joined[0], split_far)
        split_parts, _ = gather_parts(column, "dp")
        seen_inputs = after(recv_inputs, send_grads)
        seen_grads = after(recv_grads, split_parts[1])
    else:
        recv_grads = exchange(after(send_grads, recv_inputs))
        seen_inputs = after(recv_inputs, send_grads)
        seen_grads = recv_grads

    def forward_body(*refs):
        forward_kernel(rows, *refs)

    kept_inputs, hidden, slope, activation = pl.pallas_call(
        forward_body,
        in_specs=[anywhere] * 3,
        out_specs=(anywhere,) * 4,
        out_shape=(narrow_out, wide_out, wide_out, wide_out),
        scratch_shapes=[
            narrow, upright, upright, wide, wide, wide, sems(steps), sems(2), sems(4, steps),
        ],
        compiler_params=params(),
    )(seen_inputs, *in_hbm(weight_gate, weight_up))

    def delta_body(*refs):
        delta_kernel(rows, *refs)

    both, delta, kept_grads = pl.pallas_call(
        delta_body,
        in_specs=[inside] + [anywhere] * 5,
        out_specs=(inside, anywhere, anywhere),
        out_shape=(
            pltpu.VMEM((slot_count, 2 * hidden_width), bf16),
            narrow_out,
            narrow_out,
        ),
        scratch_shapes=[
            wide, wide, upright, upright, lying, narrow,
            sems(2, steps), sems(3), sems(2, steps),
        ],
        compiler_params=params(),
    )(*in_vmem(seen_grads), *in_hbm(slope, activation, weight_gate, weight_up, weight_down))
    returned = exchange(delta)

    half = group // 2
    gate_rows, down_rows = sub_width // group, hidden_width // group

    def weight_body(*refs):
        weight_kernel(group, *refs)

    grad_shapes = ((half, gate_rows, 2 * hidden_width), (half, down_rows, sub_width))
    keep_a, keep_b, send_a, send_b = pl.pallas_call(
        weight_body,
        in_specs=[anywhere, anywhere, inside, anywhere],
        out_shape=tuple(shape(dims, f32) for dims in grad_shapes)
        + tuple(shape(dims, bf16) for dims in grad_shapes),
        scratch_shapes=[
            narrow,
            narrow,
            wide,
            pltpu.VMEM((sub_width, 2 * hidden_width), f32),
            pltpu.VMEM((hidden_width, sub_width), f32),
            pltpu.SemaphoreType.DMA((3,)),
        ],
        compiler_params=params(),
        cost_estimate=cost(6 * slot_count * sub_width * hidden_width, 8 * slot_count * hidden_width),
    )(*in_hbm(kept_inputs, kept_grads), *in_vmem(both), *in_hbm(hidden))
    offset = 1
    while 2 * offset < group:
        half //= 2
        got_a, got_b = swap(send_a, "dp", offset), swap(send_b, "dp", offset)
        if in_blocks and offset == 1:
            got_b = after(got_b, split_parts[1])
        keep_a, keep_b, send_a, send_b = pl.pallas_call(
            halve_kernel,
            out_shape=(
                shape((half, gate_rows, 2 * hidden_width), f32),
                shape((half, down_rows, sub_width), f32),
                shape((half, gate_rows, 2 * hidden_width), bf16),
                shape((half, down_rows, sub_width), bf16),
            ),
            compiler_params=params(),
        )(keep_a, keep_b, got_a, got_b)
        offset *= 2
    if in_blocks:
        def interleave_body(*refs):
            interleave_kernel(dp_offsets, block_rows, refs[:-1], refs[-1])

        whole_split = pl.pallas_call(
            interleave_body,
            out_shape=pltpu.VMEM((model_width, model_width), bf16),
            compiler_params=params(),
        )(*split_parts)
        (whole_split,) = in_vmem(whole_split)
    d_tokens = pl.pallas_call(
        split_kernel,
        in_specs=[inside, anywhere, inside],
        out_shape=shape((row_count, model_width), bf16),
        scratch_shapes=[
            narrow,
            pltpu.VMEM((row_count, model_width), bf16),
            pltpu.SemaphoreType.DMA((1,)),
        ],
        compiler_params=params(),
    )(down, returned, whole_split).reshape(batch_count, tok_count, model_width)
    got_a, got_b = swap(send_a, "dp", offset), swap(send_b, "dp", offset)
    got_b = after(got_b, d_tokens)
    shared_gate, shared_up, shared_down = pl.pallas_call(
        last_kernel,
        out_shape=(
            shape((1, gate_rows, hidden_width), f32),
            shape((1, gate_rows, hidden_width), f32),
            shape((1, down_rows, sub_width), f32),
        ),
        compiler_params=params(),
    )(keep_a, keep_b, got_a, got_b)

    return (d_tokens, shared_gate, shared_up, shared_down)


def solution(mesh):
    placed = (
        P(None, ("expert", "dp"), None),
        P(None, ("expert", "dp"), None),
        P(None, ("expert", "dp"), None, None),
        P(None, ("expert", "dp"), None),
        P("expert", None),
        P("expert", None),
        P("expert", None, None),
        P("expert", None, None),
        P("expert", None, None),
    )
    return jax.shard_map(
        on_device,
        mesh=mesh,
        in_specs=placed,
        out_specs=(
            P(None, ("expert", "dp"), None),
            P("expert", "dp", None),
            P("expert", "dp", None),
            P("expert", "dp", None),
        ),
        check_vma=False,
    )
```

```python
import jax
import jax.numpy as jnp
from jax import lax
from jax.experimental import pallas as pl
from jax.experimental.pallas import tpu as pltpu
from jax.sharding import PartitionSpec as P

LANES = 128
MERGE_COST = 20000000000
ROUTE_COST = 1
GRAD_COST = 1
VMEM_BYTES = 16 * 1024 * 1024


def transposed(left_rows, right_rows):
    return lax.dot_general(
        left_rows, right_rows, (((1,), (1,)), ((), ())), preferred_element_type=jnp.float32
    )


def leading(left_rows, right_rows):
    return lax.dot_general(
        left_rows, right_rows, (((0,), (0,)), ((), ())), preferred_element_type=jnp.float32
    )


def plain(left_rows, right_rows):
    return jnp.dot(left_rows, right_rows, preferred_element_type=jnp.float32)


def power_of_two(number):
    return number & (number - 1) == 0


def swap(value, axis, offset):
    return lax.ppermute(
        value, axis, [(index, index ^ offset) for index in range(lax.axis_size(axis))]
    )


def params():
    return pltpu.CompilerParams(vmem_limit_bytes=VMEM_BYTES)


def in_hbm(*arrays):
    return [pltpu.with_memory_space_constraint(array, pltpu.HBM) for array in arrays]


def in_vmem(*arrays):
    return [pltpu.with_memory_space_constraint(array, pltpu.VMEM) for array in arrays]


def after(value, *earlier):
    return lax.optimization_barrier((value, *earlier))[0]


def cost(flops, moved):
    return pl.CostEstimate(flops=flops, bytes_accessed=moved, transcendentals=0)


def gather_blocks(block, axis, *gate):
    span = lax.axis_size(axis)
    blocks, offsets = [block], [0]
    while span > 1:
        radix = 4 if span % 4 == 0 else 2
        span //= radix
        block = jnp.concatenate(blocks) if len(blocks) > 1 else blocks[0]
        if span == 1 and gate:
            block = after(block, *gate)
        steps = [step * span for step in range(1, radix)]
        blocks = [block] + [swap(block, axis, step) for step in steps]
        offsets = offsets + [old ^ step for step in steps for old in offsets]
    return blocks, offsets


def gather_parts(block, axis):
    span = lax.axis_size(axis)
    blocks, offsets = [block], [0]
    while span > 1:
        span //= 2
        blocks = blocks + [swap(old, axis, span) for old in blocks]
        offsets = offsets + [old ^ span for old in offsets]
    return blocks, offsets


def place_rows(offsets, count, block_refs, out_ref):
    here = lax.axis_index("expert")
    held = [(ref, row) for ref in block_refs for row in range(0, ref.shape[0], count)]
    for offset, (ref, row) in zip(offsets, held):
        start = pl.multiple_of((here ^ offset) * count, count)
        out_ref[pl.ds(start, count), :] = ref[row : row + count, :]


def route_kernel(
    batch_count, slots_per, key_count, ids_ref, rows_ref, send_ref, across_ref, down_ref
):
    head_count, row_count = ids_ref.shape
    width = rows_ref.shape[1] // head_count
    lane = lax.broadcasted_iota(jnp.int32, (1, row_count), 1)
    batch = jnp.zeros((1, row_count), jnp.int32)
    for number in range(1, batch_count):
        batch = batch + (lane >= number * (row_count // batch_count)).astype(jnp.int32)
    keys = [ids_ref[head : head + 1, :] * batch_count + batch for head in range(head_count)]
    key = jnp.concatenate(keys, axis=1)
    total = head_count * row_count
    onehot = lax.broadcasted_iota(jnp.int32, (key_count, total), 0) == key
    earlier = lax.broadcasted_iota(jnp.int32, (total, total), 0) < lax.broadcasted_iota(
        jnp.int32, (total, total), 1
    )
    before = plain(
        onehot.astype(jnp.float32).astype(jnp.bfloat16),
        earlier.astype(jnp.float32).astype(jnp.bfloat16),
    )
    slot = jnp.sum(jnp.where(onehot, before, 0.0), axis=0, keepdims=True).astype(jnp.int32)
    target = key * slots_per + slot
    send_ref[...] = scatter_rows(
        target,
        [rows_ref[:, head * width : (head + 1) * width] for head in range(head_count)],
        send_ref.shape[0],
    )
    across = jnp.concatenate(
        [target[:, head * row_count : (head + 1) * row_count] for head in range(head_count)], axis=0
    )
    across_ref[...] = across
    down_ref[...] = across.astype(jnp.float32).T.astype(jnp.int32)


def scatter_rows(target, row_list, slot_count):
    total = target.shape[1]
    picked = lax.broadcasted_iota(jnp.int32, (slot_count, total), 0) == target
    return plain(
        picked.astype(jnp.float32).astype(jnp.bfloat16), jnp.concatenate(row_list, axis=0)
    ).astype(jnp.bfloat16)


def merge_kernel(offsets, count, token_refs, weight_refs, out_refs, held):
    place_rows(offsets, count, weight_refs, held)
    for token_ref, out_ref in zip(token_refs, out_refs):
        out_ref[...] = transposed(token_ref[...], held[...]).astype(jnp.bfloat16)


def assemble(offsets, part_refs, width):
    here = lax.axis_index("dp")
    parts = [ref[...].astype(jnp.float32) for ref in part_refs]
    group = len(parts)
    rows, held = parts[0].shape
    lane = lax.broadcasted_iota(jnp.int32, (rows, LANES), 1)
    blocks = []
    for expert in range(held // width):
        base = expert * width // LANES * LANES
        inside = expert * width - base
        block = jnp.zeros((rows, LANES), jnp.float32)
        for offset, part in zip(offsets, parts):
            first = (here ^ offset) * width
            shift = lax.rem(first + LANES - inside, LANES)
            moved = pltpu.roll(part[:, base : base + LANES], shift, 1)
            block = jnp.where((lane >= first) & (lane < first + width), moved, block)
        blocks.append(block)
    return jnp.concatenate(blocks, axis=1)


def grad_kernel(offsets, width, scale_ref, across_ref, *rest):
    part_refs, send_ref = rest[:-1], rest[-1]
    merged = (
        part_refs[0][...].astype(jnp.float32)
        if offsets is None
        else assemble(offsets, part_refs, width)
    )
    head_count = across_ref.shape[0]
    sub_width = merged.shape[1] // head_count
    rows = [
        (
            scale_ref[:, head : head + 1] * merged[:, head * sub_width : (head + 1) * sub_width]
        ).astype(jnp.bfloat16)
        for head in range(head_count)
    ]
    target = jnp.concatenate([across_ref[head : head + 1, :] for head in range(head_count)], axis=1)
    send_ref[...] = scatter_rows(target, rows, send_ref.shape[0])


def chunks(count, chunk):
    return [slice(start, start + chunk) for start in range(0, count, chunk)]


def fetch(source_ref, held_ref, sems, rows):
    copies = [
        pltpu.make_async_copy(source_ref.at[part, :], held_ref.at[part, :], sems.at[number])
        for number, part in enumerate(rows)
    ]
    for copy in copies:
        copy.start()
    return copies


def send_out(source_ref, target_ref, part, sem):
    copy = pltpu.make_async_copy(source_ref.at[part, :], target_ref.at[part, :], sem)
    copy.start()
    return copy


def forward_kernel(
    rows, input_ref, gate_ref, up_ref, inputs_out, hidden_out, slope_out, activation_out,
    inputs_held, gate_held, up_held, hidden, slope, activation_held, sems, weight_sems, out_sems
):
    copies = fetch(input_ref, inputs_held, sems, rows)
    weights = [
        pltpu.make_async_copy(gate_ref, gate_held, weight_sems.at[0]),
        pltpu.make_async_copy(up_ref, up_held, weight_sems.at[1]),
    ]
    for copy in weights:
        copy.start()
    for copy in weights:
        copy.wait()
    outs = []
    for number, (part, copy) in enumerate(zip(rows, copies)):
        copy.wait()
        inputs = inputs_held[part, :]
        pre_gate = plain(inputs, gate_held[...])
        pre_up = plain(inputs, up_held[...])
        sigma = jax.nn.sigmoid(pre_gate)
        activation = pre_gate * sigma
        slope_value = sigma * (1.0 + pre_gate * (1.0 - sigma))
        hidden[part, :] = (activation * pre_up).astype(jnp.bfloat16)
        slope[part, :] = (pre_up * slope_value).astype(jnp.bfloat16)
        activation_held[part, :] = activation.astype(jnp.bfloat16)
        for place, (source, target) in enumerate(
            (
                (inputs_held, inputs_out),
                (hidden, hidden_out),
                (slope, slope_out),
                (activation_held, activation_out),
            )
        ):
            outs.append(send_out(source, target, part, out_sems.at[place, number]))
    for copy in outs:
        copy.wait()


def delta_kernel(
    rows, grad_ref, slope_ref, activation_ref, gate_ref, up_ref, down_ref,
    both_ref, delta_ref, grads_out,
    grads_held, slope, activation, gate_held, up_held, down_held, out, sems, weight_sems, out_sems
):
    hidden_width = gate_ref.shape[1]
    weights = [
        pltpu.make_async_copy(source, target, weight_sems.at[number])
        for number, (source, target) in enumerate(
            ((down_ref, down_held), (gate_ref, gate_held), (up_ref, up_held))
        )
    ]
    arriving = {}

    def bring(number):
        if number < len(rows):
            arriving[number] = [
                send_out(source, target, rows[number], sems.at[place, number])
                for place, (source, target) in enumerate(
                    ((grad_ref, grads_held), (slope_ref, slope), (activation_ref, activation))
                )
            ]

    weights[0].start()
    bring(0)
    weights[1].start()
    weights[2].start()
    weights[0].wait()
    outs = []
    for number, part in enumerate(rows):
        arriving[number][0].wait()
        d_hidden = transposed(grads_held[part, :], down_held[...])
        arriving[number][1].wait()
        arriving[number][2].wait()
        if number == 0:
            bring(1)
            bring(2)
        else:
            bring(number + 2)
        delta_gate = (d_hidden * slope[part, :].astype(jnp.float32)).astype(jnp.bfloat16)
        delta_up = (d_hidden * activation[part, :].astype(jnp.float32)).astype(jnp.bfloat16)
        both_ref[part, :hidden_width] = delta_gate
        both_ref[part, hidden_width:] = delta_up
        if number == 0:
            weights[1].wait()
            weights[2].wait()
        out[part, :] = (
            transposed(delta_gate, gate_held[...]) + transposed(delta_up, up_held[...])
        ).astype(jnp.bfloat16)
        outs.append(send_out(out, delta_ref, part, out_sems.at[0, number]))
        outs.append(send_out(grads_held, grads_out, part, out_sems.at[1, number]))
    for copy in outs:
        copy.wait()


def weight_kernel(
    group, input_ref, grad_ref, both_ref, hidden_ref, keep_a, keep_b, send_a, send_b,
    inputs_held, grads_held, hidden_held, held_a, held_b, sems
):
    here = lax.axis_index("dp")
    copies = [
        pltpu.make_async_copy(source, target, sems.at[number])
        for number, (source, target) in enumerate(
            ((input_ref, inputs_held), (grad_ref, grads_held), (hidden_ref, hidden_held))
        )
    ]
    for copy in copies:
        copy.start()
    copies[0].wait()
    held_a[...] = leading(inputs_held[...], both_ref[...])
    copies[1].wait()
    copies[2].wait()
    held_b[...] = leading(hidden_held[...], grads_held[...])
    give_weights(group, here, held_a, held_b, keep_a, keep_b, send_a, send_b)


def give_weights(group, here, held_a, held_b, keep_a, keep_b, send_a, send_b):
    for held, keep, send in ((held_a, keep_a, send_a), (held_b, keep_b, send_b)):
        rows = held.shape[0] // group
        for place in range(group // 2):
            own = pl.multiple_of((here ^ (2 * place)) * rows, rows)
            keep[place] = held[pl.ds(own, rows), :]
            other = pl.multiple_of((here ^ (2 * place + 1)) * rows, rows)
            send[place] = held[pl.ds(other, rows), :].astype(jnp.bfloat16)


def halve_kernel(keep_a, keep_b, got_a, got_b, next_a, next_b, send_a, send_b):
    for keep, got, own, send in (
        (keep_a, got_a, next_a, send_a),
        (keep_b, got_b, next_b, send_b),
    ):
        count = own.shape[0]
        for place in range(count):
            own[place] = keep[2 * place] + got[2 * place].astype(jnp.float32)
            send[place] = (keep[2 * place + 1] + got[2 * place + 1].astype(jnp.float32)).astype(
                jnp.bfloat16
            )


def last_kernel(keep_a, keep_b, got_a, got_b, gate_ref, up_ref, down_ref):
    width = gate_ref.shape[2]
    summed = keep_a[0] + got_a[0].astype(jnp.float32)
    gate_ref[0] = summed[:, :width]
    up_ref[0] = summed[:, width:]
    down_ref[0] = keep_b[0] + got_b[0].astype(jnp.float32)


def interleave_kernel(offsets, count, part_refs, out_ref):
    here = lax.axis_index("dp")
    for offset, part_ref in zip(offsets, part_refs):
        for place in range(part_ref.shape[0] // count):
            start = (place * len(offsets) + (here ^ offset)) * count
            out_ref[pl.ds(pl.multiple_of(start, count), count), :] = part_ref[
                place * count : (place + 1) * count, :
            ]


def split_kernel(down_ref, back_ref, weight_ref, out_ref, back, held, sems):
    row_count, head_count = down_ref.shape
    slot_count, width = back_ref.shape
    (copy,) = fetch(back_ref, back, sems, [slice(0, slot_count)])
    lane = lax.broadcasted_iota(jnp.int32, (row_count, slot_count), 1)
    picked = jnp.concatenate(
        [
            (lane == down_ref[:, head : head + 1]).astype(jnp.float32).astype(jnp.bfloat16)
            for head in range(head_count)
        ],
        axis=0,
    )
    copy.wait()
    rows = plain(picked, back[...]).astype(jnp.bfloat16)
    for head in range(head_count):
        held[:, head * width : (head + 1) * width] = rows[head * row_count : (head + 1) * row_count]
    out_ref[...] = transposed(held[...], weight_ref[...]).astype(jnp.bfloat16)


def on_device(
    out_grad,
    sub_inputs,
    route,
    gate_scale,
    merge_weight,
    split_weight,
    expert_gate,
    expert_up,
    expert_down,
):
    batch_count, tok_count, model_width = out_grad.shape
    head_count = route.shape[2]
    sub_width = model_width // head_count
    expert_count = lax.axis_size("expert")
    group = lax.axis_size("dp")
    here = lax.axis_index("dp")
    slots_per = 2 * tok_count * head_count // expert_count
    row_count = batch_count * tok_count
    key_count = expert_count * batch_count
    slot_count = key_count * slots_per
    shard_rows = merge_weight.shape[0]
    hidden_width = expert_gate.shape[2]
    bf16, f32 = jnp.bfloat16, jnp.float32
    block_rows = shard_rows // group
    in_blocks = (
        shard_rows == LANES
        and block_rows % 16 == 0
        and power_of_two(expert_count)
        and power_of_two(group)
    )
    shape = jax.ShapeDtypeStruct
    tokens = out_grad.reshape(row_count, model_width)
    rows_in = sub_inputs.reshape(row_count, model_width)
    scale = gate_scale.reshape(row_count, head_count)
    ids = route.reshape(row_count, head_count).T

    if in_blocks:
        own_block = lambda weight: lax.dynamic_slice_in_dim(
            weight, here * block_rows, block_rows, 0
        )
        pair = jnp.stack([own_block(merge_weight), own_block(split_weight)])
        pairs = [pair] + [swap(pair, "expert", step * (expert_count // 4)) for step in range(1, 4)]
        merge_joined = jnp.concatenate([one[0] for one in pairs])
        split_joined = [jnp.concatenate([one[1] for one in pairs])]
        merge_blocks = [merge_joined, swap(merge_joined, "expert", 1)]
        offsets = [0, 2, 4, 6, 1, 3, 5, 7]
        ids = after(ids, pairs[1])

    def route_body(*refs):
        route_kernel(batch_count, slots_per, key_count, *refs)

    send_inputs, across, down = pl.pallas_call(
        route_body,
        out_shape=(
            shape((slot_count, sub_width), bf16),
            shape((head_count, row_count), jnp.int32),
            shape((row_count, head_count), jnp.int32),
        ),
        compiler_params=params(),
        cost_estimate=cost(ROUTE_COST, 1),
    )(ids, *in_hbm(rows_in))

    if in_blocks:
        token_parts, dp_offsets = gather_parts(after(tokens, across), "dp")
    else:
        whole_merge = lax.all_gather(merge_weight, "expert", axis=0, tiled=True)
        whole_split = lax.all_gather(split_weight, "expert", axis=0, tiled=True)

    def exchange(rows):
        return lax.all_to_all(
            rows.reshape(expert_count, -1, sub_width), "expert", 0, 0, tiled=True
        ).reshape(slot_count, sub_width)

    recv_inputs = exchange(send_inputs)

    if in_blocks:

        def merge_body(*refs):
            last = group + len(merge_blocks)
            merge_kernel(
                offsets, block_rows, refs[:group], refs[group:last], refs[last:-1], refs[-1]
            )

        part_width = expert_count * block_rows
        parts = pl.pallas_call(
            merge_body,
            out_shape=tuple(shape((row_count, part_width), bf16) for _ in range(group)),
            scratch_shapes=[pltpu.VMEM((part_width, model_width), bf16)],
            compiler_params=params(),
            cost_estimate=cost(MERGE_COST, 1),
        )(*token_parts, *merge_blocks)
        parts = [
            part if offset == 0 else swap(part, "dp", offset)
            for part, offset in zip(parts, dp_offsets)
        ]
    else:
        dp_offsets = None
        parts = [transposed(tokens, whole_merge).astype(bf16)]

    def grad_body(*refs):
        grad_kernel(dp_offsets, block_rows, *refs)

    send_grads = pl.pallas_call(
        grad_body,
        out_shape=shape((slot_count, sub_width), bf16),
        compiler_params=params(),
        cost_estimate=cost(GRAD_COST, 1),
    )(scale, across, *parts)
    weight_gate = expert_gate[0]
    weight_up = expert_up[0]
    weight_down = expert_down[0]
    rows = chunks(slot_count, slot_count // 2)
    anywhere = pl.BlockSpec(memory_space=pl.ANY)
    inside = pl.BlockSpec(memory_space=pltpu.VMEM)
    wide = pltpu.VMEM((slot_count, hidden_width), bf16)
    narrow = pltpu.VMEM((slot_count, sub_width), bf16)
    upright = pltpu.VMEM(weight_gate.shape, bf16)
    lying = pltpu.VMEM(weight_down.shape, bf16)
    sems = lambda *dims: pltpu.SemaphoreType.DMA(dims)
    steps = len(rows)
    wide_out = pltpu.HBM((slot_count, hidden_width), bf16)
    narrow_out = pltpu.HBM((slot_count, sub_width), bf16)

    if in_blocks:
        split_far = swap(after(split_joined[0], parts[0]), "expert", 1)
        recv_grads = exchange(after(send_grads, recv_inputs, split_far))

        def order_body(*refs):
            place_rows(offsets, block_rows, refs[:-1], refs[-1])

        column = pl.pallas_call(
            order_body,
            out_shape=shape((part_width, model_width), bf16),
            compiler_params=params(),
        )(split_joined[0], split_far)
        split_parts, _ = gather_parts(column, "dp")
        seen_inputs = after(recv_inputs, send_grads)
        seen_grads = after(recv_grads, split_parts[1])
    else:
        recv_grads = exchange(after(send_grads, recv_inputs))
        seen_inputs = after(recv_inputs, send_grads)
        seen_grads = recv_grads

    def forward_body(*refs):
        forward_kernel(rows, *refs)

    kept_inputs, hidden, slope, activation = pl.pallas_call(
        forward_body,
        in_specs=[anywhere] * 3,
        out_specs=(anywhere,) * 4,
        out_shape=(narrow_out, wide_out, wide_out, wide_out),
        scratch_shapes=[
            narrow, upright, upright, wide, wide, wide, sems(steps), sems(2), sems(4, steps),
        ],
        compiler_params=params(),
    )(seen_inputs, *in_hbm(weight_gate, weight_up))

    def delta_body(*refs):
        delta_kernel(rows, *refs)

    both, delta, kept_grads = pl.pallas_call(
        delta_body,
        in_specs=[anywhere] * 6,
        out_specs=(inside, anywhere, anywhere),
        out_shape=(
            pltpu.VMEM((slot_count, 2 * hidden_width), bf16),
            narrow_out,
            narrow_out,
        ),
        scratch_shapes=[
            narrow, wide, wide, upright, upright, lying, narrow,
            sems(3, steps), sems(3), sems(2, steps),
        ],
        compiler_params=params(),
    )(*in_hbm(seen_grads), *in_hbm(slope, activation, weight_gate, weight_up, weight_down))
    returned = exchange(delta)

    half = group // 2
    gate_rows, down_rows = sub_width // group, hidden_width // group

    def weight_body(*refs):
        weight_kernel(group, *refs)

    grad_shapes = ((half, gate_rows, 2 * hidden_width), (half, down_rows, sub_width))
    keep_a, keep_b, send_a, send_b = pl.pallas_call(
        weight_body,
        in_specs=[anywhere, anywhere, inside, anywhere],
        out_shape=tuple(shape(dims, f32) for dims in grad_shapes)
        + tuple(shape(dims, bf16) for dims in grad_shapes),
        scratch_shapes=[
            narrow,
            narrow,
            wide,
            pltpu.VMEM((sub_width, 2 * hidden_width), f32),
            pltpu.VMEM((hidden_width, sub_width), f32),
            pltpu.SemaphoreType.DMA((3,)),
        ],
        compiler_params=params(),
        cost_estimate=cost(6 * slot_count * sub_width * hidden_width, 8 * slot_count * hidden_width),
    )(*in_hbm(kept_inputs, kept_grads), *in_vmem(both), *in_hbm(hidden))
    offset = 1
    while 2 * offset < group:
        half //= 2
        got_a, got_b = swap(send_a, "dp", offset), swap(send_b, "dp", offset)
        if in_blocks and offset == 1:
            got_b = after(got_b, split_parts[1])
        keep_a, keep_b, send_a, send_b = pl.pallas_call(
            halve_kernel,
            out_shape=(
                shape((half, gate_rows, 2 * hidden_width), f32),
                shape((half, down_rows, sub_width), f32),
                shape((half, gate_rows, 2 * hidden_width), bf16),
                shape((half, down_rows, sub_width), bf16),
            ),
            compiler_params=params(),
        )(keep_a, keep_b, got_a, got_b)
        offset *= 2
    if in_blocks:
        def interleave_body(*refs):
            interleave_kernel(dp_offsets, block_rows, refs[:-1], refs[-1])

        whole_split = pl.pallas_call(
            interleave_body,
            out_shape=pltpu.VMEM((model_width, model_width), bf16),
            compiler_params=params(),
        )(*split_parts)
        (whole_split,) = in_vmem(whole_split)
    d_tokens = pl.pallas_call(
        split_kernel,
        in_specs=[inside, anywhere, inside],
        out_shape=shape((row_count, model_width), bf16),
        scratch_shapes=[
            narrow,
            pltpu.VMEM((row_count, model_width), bf16),
            pltpu.SemaphoreType.DMA((1,)),
        ],
        compiler_params=params(),
    )(down, returned, whole_split).reshape(batch_count, tok_count, model_width)
    got_a, got_b = swap(send_a, "dp", offset), swap(send_b, "dp", offset)
    got_b = after(got_b, d_tokens)
    shared_gate, shared_up, shared_down = pl.pallas_call(
        last_kernel,
        out_shape=(
            shape((1, gate_rows, hidden_width), f32),
            shape((1, gate_rows, hidden_width), f32),
            shape((1, down_rows, sub_width), f32),
        ),
        compiler_params=params(),
    )(keep_a, keep_b, got_a, got_b)

    return (d_tokens, shared_gate, shared_up, shared_down)


def solution(mesh):
    placed = (
        P(None, ("expert", "dp"), None),
        P(None, ("expert", "dp"), None),
        P(None, ("expert", "dp"), None, None),
        P(None, ("expert", "dp"), None),
        P("expert", None),
        P("expert", None),
        P("expert", None, None),
        P("expert", None, None),
        P("expert", None, None),
    )
    return jax.shard_map(
        on_device,
        mesh=mesh,
        in_specs=placed,
        out_specs=(
            P(None, ("expert", "dp"), None),
            P("expert", "dp", None),
            P("expert", "dp", None),
            P("expert", "dp", None),
        ),
        check_vma=False,
    )
```

```python
import jax
import jax.numpy as jnp
from jax import lax
from jax.experimental import pallas as pl
from jax.experimental.pallas import tpu as pltpu
from jax.sharding import PartitionSpec as P

LANES = 128
MERGE_COST = 20000000000
ROUTE_COST = 1
GRAD_COST = 1
VMEM_BYTES = 16 * 1024 * 1024


def transposed(left_rows, right_rows):
    return lax.dot_general(
        left_rows, right_rows, (((1,), (1,)), ((), ())), preferred_element_type=jnp.float32
    )


def leading(left_rows, right_rows):
    return lax.dot_general(
        left_rows, right_rows, (((0,), (0,)), ((), ())), preferred_element_type=jnp.float32
    )


def plain(left_rows, right_rows):
    return jnp.dot(left_rows, right_rows, preferred_element_type=jnp.float32)


def power_of_two(number):
    return number & (number - 1) == 0


def swap(value, axis, offset):
    return lax.ppermute(
        value, axis, [(index, index ^ offset) for index in range(lax.axis_size(axis))]
    )


def params():
    return pltpu.CompilerParams(vmem_limit_bytes=VMEM_BYTES)


def in_hbm(*arrays):
    return [pltpu.with_memory_space_constraint(array, pltpu.HBM) for array in arrays]


def in_vmem(*arrays):
    return [pltpu.with_memory_space_constraint(array, pltpu.VMEM) for array in arrays]


def after(value, *earlier):
    return lax.optimization_barrier((value, *earlier))[0]


def cost(flops, moved):
    return pl.CostEstimate(flops=flops, bytes_accessed=moved, transcendentals=0)


def gather_blocks(block, axis, *gate):
    span = lax.axis_size(axis)
    blocks, offsets = [block], [0]
    while span > 1:
        radix = 4 if span % 4 == 0 else 2
        span //= radix
        block = jnp.concatenate(blocks) if len(blocks) > 1 else blocks[0]
        if span == 1 and gate:
            block = after(block, *gate)
        steps = [step * span for step in range(1, radix)]
        blocks = [block] + [swap(block, axis, step) for step in steps]
        offsets = offsets + [old ^ step for step in steps for old in offsets]
    return blocks, offsets


def gather_parts(block, axis):
    span = lax.axis_size(axis)
    blocks, offsets = [block], [0]
    while span > 1:
        span //= 2
        blocks = blocks + [swap(old, axis, span) for old in blocks]
        offsets = offsets + [old ^ span for old in offsets]
    return blocks, offsets


def place_rows(offsets, count, block_refs, out_ref):
    here = lax.axis_index("expert")
    held = [(ref, row) for ref in block_refs for row in range(0, ref.shape[0], count)]
    for offset, (ref, row) in zip(offsets, held):
        start = pl.multiple_of((here ^ offset) * count, count)
        out_ref[pl.ds(start, count), :] = ref[row : row + count, :]


def route_kernel(
    batch_count, slots_per, key_count, ids_ref, rows_ref, send_ref, across_ref, down_ref
):
    head_count, row_count = ids_ref.shape
    width = rows_ref.shape[1] // head_count
    lane = lax.broadcasted_iota(jnp.int32, (1, row_count), 1)
    batch = jnp.zeros((1, row_count), jnp.int32)
    for number in range(1, batch_count):
        batch = batch + (lane >= number * (row_count // batch_count)).astype(jnp.int32)
    keys = [ids_ref[head : head + 1, :] * batch_count + batch for head in range(head_count)]
    key = jnp.concatenate(keys, axis=1)
    total = head_count * row_count
    onehot = lax.broadcasted_iota(jnp.int32, (key_count, total), 0) == key
    earlier = lax.broadcasted_iota(jnp.int32, (total, total), 0) < lax.broadcasted_iota(
        jnp.int32, (total, total), 1
    )
    before = plain(
        onehot.astype(jnp.float32).astype(jnp.bfloat16),
        earlier.astype(jnp.float32).astype(jnp.bfloat16),
    )
    slot = jnp.sum(jnp.where(onehot, before, 0.0), axis=0, keepdims=True).astype(jnp.int32)
    target = key * slots_per + slot
    send_ref[...] = scatter_rows(
        target,
        [rows_ref[:, head * width : (head + 1) * width] for head in range(head_count)],
        send_ref.shape[0],
    )
    across = jnp.concatenate(
        [target[:, head * row_count : (head + 1) * row_count] for head in range(head_count)], axis=0
    )
    across_ref[...] = across
    down_ref[...] = across.astype(jnp.float32).T.astype(jnp.int32)


def scatter_rows(target, row_list, slot_count):
    total = target.shape[1]
    picked = lax.broadcasted_iota(jnp.int32, (slot_count, total), 0) == target
    return plain(
        picked.astype(jnp.float32).astype(jnp.bfloat16), jnp.concatenate(row_list, axis=0)
    ).astype(jnp.bfloat16)


def merge_kernel(offsets, count, token_refs, weight_refs, out_refs, held):
    place_rows(offsets, count, weight_refs, held)
    for token_ref, out_ref in zip(token_refs, out_refs):
        out_ref[...] = transposed(token_ref[...], held[...]).astype(jnp.bfloat16)


def assemble(offsets, part_refs, width):
    here = lax.axis_index("dp")
    parts = [ref[...].astype(jnp.float32) for ref in part_refs]
    group = len(parts)
    rows, held = parts[0].shape
    lane = lax.broadcasted_iota(jnp.int32, (rows, LANES), 1)
    blocks = []
    for expert in range(held // width):
        base = expert * width // LANES * LANES
        inside = expert * width - base
        block = jnp.zeros((rows, LANES), jnp.float32)
        for offset, part in zip(offsets, parts):
            first = (here ^ offset) * width
            shift = lax.rem(first + LANES - inside, LANES)
            moved = pltpu.roll(part[:, base : base + LANES], shift, 1)
            block = jnp.where((lane >= first) & (lane < first + width), moved, block)
        blocks.append(block)
    return jnp.concatenate(blocks, axis=1)


def grad_kernel(offsets, width, scale_ref, across_ref, *rest):
    part_refs, send_ref = rest[:-1], rest[-1]
    merged = (
        part_refs[0][...].astype(jnp.float32)
        if offsets is None
        else assemble(offsets, part_refs, width)
    )
    head_count = across_ref.shape[0]
    sub_width = merged.shape[1] // head_count
    rows = [
        (
            scale_ref[:, head : head + 1] * merged[:, head * sub_width : (head + 1) * sub_width]
        ).astype(jnp.bfloat16)
        for head in range(head_count)
    ]
    target = jnp.concatenate([across_ref[head : head + 1, :] for head in range(head_count)], axis=1)
    send_ref[...] = scatter_rows(target, rows, send_ref.shape[0])


def chunks(count, chunk):
    return [slice(start, start + chunk) for start in range(0, count, chunk)]


def fetch(source_ref, held_ref, sems, rows):
    copies = [
        pltpu.make_async_copy(source_ref.at[part, :], held_ref.at[part, :], sems.at[number])
        for number, part in enumerate(rows)
    ]
    for copy in copies:
        copy.start()
    return copies


def send_out(source_ref, target_ref, part, sem):
    copy = pltpu.make_async_copy(source_ref.at[part, :], target_ref.at[part, :], sem)
    copy.start()
    return copy


def forward_kernel(
    rows, input_ref, gate_ref, up_ref, down_ref, inputs_out, hidden_out, slope_out, activation_out,
    down_held, inputs_held, gate_held, up_held, hidden, slope, activation_held, sems, weight_sems, out_sems
):
    copies = fetch(input_ref, inputs_held, sems, rows)
    weights = [
        pltpu.make_async_copy(gate_ref, gate_held, weight_sems.at[0]),
        pltpu.make_async_copy(up_ref, up_held, weight_sems.at[1]),
    ]
    down_copy = pltpu.make_async_copy(down_ref, down_held, weight_sems.at[2])
    for copy in weights:
        copy.start()
    down_copy.start()
    for copy in weights:
        copy.wait()
    outs = []
    for number, (part, copy) in enumerate(zip(rows, copies)):
        copy.wait()
        inputs = inputs_held[part, :]
        pre_gate = plain(inputs, gate_held[...])
        pre_up = plain(inputs, up_held[...])
        sigma = jax.nn.sigmoid(pre_gate)
        activation = pre_gate * sigma
        slope_value = sigma * (1.0 + pre_gate * (1.0 - sigma))
        hidden[part, :] = (activation * pre_up).astype(jnp.bfloat16)
        slope[part, :] = (pre_up * slope_value).astype(jnp.bfloat16)
        activation_held[part, :] = activation.astype(jnp.bfloat16)
        for place, (source, target) in enumerate(
            (
                (inputs_held, inputs_out),
                (hidden, hidden_out),
                (slope, slope_out),
                (activation_held, activation_out),
            )
        ):
            outs.append(send_out(source, target, part, out_sems.at[place, number]))
    down_copy.wait()
    for copy in outs:
        copy.wait()


def delta_kernel(
    rows, grad_ref, slope_ref, activation_ref, gate_ref, up_ref, down_held,
    both_ref, delta_ref, grads_out,
    grads_held, slope, activation, gate_held, up_held, out, sems, weight_sems, out_sems
):
    hidden_width = gate_ref.shape[1]
    weights = [
        pltpu.make_async_copy(source, target, weight_sems.at[number])
        for number, (source, target) in enumerate(
            ((gate_ref, gate_held), (up_ref, up_held))
        )
    ]
    arriving = {}

    def bring(number):
        if number < len(rows):
            arriving[number] = [
                send_out(source, target, rows[number], sems.at[place, number])
                for place, (source, target) in enumerate(
                    ((grad_ref, grads_held), (slope_ref, slope), (activation_ref, activation))
                )
            ]

    bring(0)
    weights[0].start()
    weights[1].start()
    outs = []
    for number, part in enumerate(rows):
        arriving[number][0].wait()
        d_hidden = transposed(grads_held[part, :], down_held[...])
        arriving[number][1].wait()
        arriving[number][2].wait()
        if number == 0:
            bring(1)
            bring(2)
        else:
            bring(number + 2)
        delta_gate = (d_hidden * slope[part, :].astype(jnp.float32)).astype(jnp.bfloat16)
        delta_up = (d_hidden * activation[part, :].astype(jnp.float32)).astype(jnp.bfloat16)
        both_ref[part, :hidden_width] = delta_gate
        both_ref[part, hidden_width:] = delta_up
        if number == 0:
            weights[0].wait()
            weights[1].wait()
        out[part, :] = (
            transposed(delta_gate, gate_held[...]) + transposed(delta_up, up_held[...])
        ).astype(jnp.bfloat16)
        outs.append(send_out(out, delta_ref, part, out_sems.at[0, number]))
        outs.append(send_out(grads_held, grads_out, part, out_sems.at[1, number]))
    for copy in outs:
        copy.wait()


def weight_kernel(
    group, input_ref, grad_ref, both_ref, hidden_ref, keep_a, keep_b, send_a, send_b,
    inputs_held, grads_held, hidden_held, held_a, held_b, sems
):
    here = lax.axis_index("dp")
    copies = [
        pltpu.make_async_copy(source, target, sems.at[number])
        for number, (source, target) in enumerate(
            ((input_ref, inputs_held), (grad_ref, grads_held), (hidden_ref, hidden_held))
        )
    ]
    for copy in copies:
        copy.start()
    copies[0].wait()
    held_a[...] = leading(inputs_held[...], both_ref[...])
    copies[1].wait()
    copies[2].wait()
    held_b[...] = leading(hidden_held[...], grads_held[...])
    give_weights(group, here, held_a, held_b, keep_a, keep_b, send_a, send_b)


def give_weights(group, here, held_a, held_b, keep_a, keep_b, send_a, send_b):
    for held, keep, send in ((held_a, keep_a, send_a), (held_b, keep_b, send_b)):
        rows = held.shape[0] // group
        for place in range(group // 2):
            own = pl.multiple_of((here ^ (2 * place)) * rows, rows)
            keep[place] = held[pl.ds(own, rows), :]
            other = pl.multiple_of((here ^ (2 * place + 1)) * rows, rows)
            send[place] = held[pl.ds(other, rows), :].astype(jnp.bfloat16)


def halve_kernel(keep_a, keep_b, got_a, got_b, next_a, next_b, send_a, send_b):
    for keep, got, own, send in (
        (keep_a, got_a, next_a, send_a),
        (keep_b, got_b, next_b, send_b),
    ):
        count = own.shape[0]
        for place in range(count):
            own[place] = keep[2 * place] + got[2 * place].astype(jnp.float32)
            send[place] = (keep[2 * place + 1] + got[2 * place + 1].astype(jnp.float32)).astype(
                jnp.bfloat16
            )


def last_kernel(keep_a, keep_b, got_a, got_b, gate_ref, up_ref, down_ref):
    width = gate_ref.shape[2]
    summed = keep_a[0] + got_a[0].astype(jnp.float32)
    gate_ref[0] = summed[:, :width]
    up_ref[0] = summed[:, width:]
    down_ref[0] = keep_b[0] + got_b[0].astype(jnp.float32)


def interleave_kernel(offsets, count, part_refs, out_ref):
    here = lax.axis_index("dp")
    for offset, part_ref in zip(offsets, part_refs):
        for place in range(part_ref.shape[0] // count):
            start = (place * len(offsets) + (here ^ offset)) * count
            out_ref[pl.ds(pl.multiple_of(start, count), count), :] = part_ref[
                place * count : (place + 1) * count, :
            ]


def split_kernel(down_ref, back_ref, weight_ref, out_ref, back, held, sems):
    row_count, head_count = down_ref.shape
    slot_count, width = back_ref.shape
    (copy,) = fetch(back_ref, back, sems, [slice(0, slot_count)])
    lane = lax.broadcasted_iota(jnp.int32, (row_count, slot_count), 1)
    picked = jnp.concatenate(
        [
            (lane == down_ref[:, head : head + 1]).astype(jnp.float32).astype(jnp.bfloat16)
            for head in range(head_count)
        ],
        axis=0,
    )
    copy.wait()
    rows = plain(picked, back[...]).astype(jnp.bfloat16)
    for head in range(head_count):
        held[:, head * width : (head + 1) * width] = rows[head * row_count : (head + 1) * row_count]
    out_ref[...] = transposed(held[...], weight_ref[...]).astype(jnp.bfloat16)


def on_device(
    out_grad,
    sub_inputs,
    route,
    gate_scale,
    merge_weight,
    split_weight,
    expert_gate,
    expert_up,
    expert_down,
):
    batch_count, tok_count, model_width = out_grad.shape
    head_count = route.shape[2]
    sub_width = model_width // head_count
    expert_count = lax.axis_size("expert")
    group = lax.axis_size("dp")
    here = lax.axis_index("dp")
    slots_per = 2 * tok_count * head_count // expert_count
    row_count = batch_count * tok_count
    key_count = expert_count * batch_count
    slot_count = key_count * slots_per
    shard_rows = merge_weight.shape[0]
    hidden_width = expert_gate.shape[2]
    bf16, f32 = jnp.bfloat16, jnp.float32
    block_rows = shard_rows // group
    in_blocks = (
        shard_rows == LANES
        and block_rows % 16 == 0
        and power_of_two(expert_count)
        and power_of_two(group)
    )
    shape = jax.ShapeDtypeStruct
    tokens = out_grad.reshape(row_count, model_width)
    rows_in = sub_inputs.reshape(row_count, model_width)
    scale = gate_scale.reshape(row_count, head_count)
    ids = route.reshape(row_count, head_count).T

    if in_blocks:
        own_block = lambda weight: lax.dynamic_slice_in_dim(
            weight, here * block_rows, block_rows, 0
        )
        pair = jnp.stack([own_block(merge_weight), own_block(split_weight)])
        pairs = [pair] + [swap(pair, "expert", step * (expert_count // 4)) for step in range(1, 4)]
        merge_joined = jnp.concatenate([one[0] for one in pairs])
        split_joined = [jnp.concatenate([one[1] for one in pairs])]
        merge_blocks = [merge_joined, swap(merge_joined, "expert", 1)]
        offsets = [0, 2, 4, 6, 1, 3, 5, 7]
        ids = after(ids, pairs[1])

    def route_body(*refs):
        route_kernel(batch_count, slots_per, key_count, *refs)

    send_inputs, across, down = pl.pallas_call(
        route_body,
        out_shape=(
            shape((slot_count, sub_width), bf16),
            shape((head_count, row_count), jnp.int32),
            shape((row_count, head_count), jnp.int32),
        ),
        compiler_params=params(),
        cost_estimate=cost(ROUTE_COST, 1),
    )(ids, *in_hbm(rows_in))

    if in_blocks:
        token_parts, dp_offsets = gather_parts(after(tokens, across), "dp")
    else:
        whole_merge = lax.all_gather(merge_weight, "expert", axis=0, tiled=True)
        whole_split = lax.all_gather(split_weight, "expert", axis=0, tiled=True)

    def exchange(rows):
        return lax.all_to_all(
            rows.reshape(expert_count, -1, sub_width), "expert", 0, 0, tiled=True
        ).reshape(slot_count, sub_width)

    recv_inputs = exchange(send_inputs)

    if in_blocks:

        def merge_body(*refs):
            last = group + len(merge_blocks)
            merge_kernel(
                offsets, block_rows, refs[:group], refs[group:last], refs[last:-1], refs[-1]
            )

        part_width = expert_count * block_rows
        parts = pl.pallas_call(
            merge_body,
            out_shape=tuple(shape((row_count, part_width), bf16) for _ in range(group)),
            scratch_shapes=[pltpu.VMEM((part_width, model_width), bf16)],
            compiler_params=params(),
            cost_estimate=cost(MERGE_COST, 1),
        )(*token_parts, *merge_blocks)
        parts = [
            part if offset == 0 else swap(part, "dp", offset)
            for part, offset in zip(parts, dp_offsets)
        ]
    else:
        dp_offsets = None
        parts = [transposed(tokens, whole_merge).astype(bf16)]

    def grad_body(*refs):
        grad_kernel(dp_offsets, block_rows, *refs)

    send_grads = pl.pallas_call(
        grad_body,
        out_shape=shape((slot_count, sub_width), bf16),
        compiler_params=params(),
        cost_estimate=cost(GRAD_COST, 1),
    )(scale, across, *parts)
    weight_gate = expert_gate[0]
    weight_up = expert_up[0]
    weight_down = expert_down[0]
    rows = chunks(slot_count, slot_count // 2)
    anywhere = pl.BlockSpec(memory_space=pl.ANY)
    inside = pl.BlockSpec(memory_space=pltpu.VMEM)
    wide = pltpu.VMEM((slot_count, hidden_width), bf16)
    narrow = pltpu.VMEM((slot_count, sub_width), bf16)
    upright = pltpu.VMEM(weight_gate.shape, bf16)
    lying = pltpu.VMEM(weight_down.shape, bf16)
    sems = lambda *dims: pltpu.SemaphoreType.DMA(dims)
    steps = len(rows)
    wide_out = pltpu.HBM((slot_count, hidden_width), bf16)
    narrow_out = pltpu.HBM((slot_count, sub_width), bf16)

    if in_blocks:
        split_far = swap(after(split_joined[0], parts[0]), "expert", 1)
        recv_grads = exchange(after(send_grads, recv_inputs, split_far))

        def order_body(*refs):
            place_rows(offsets, block_rows, refs[:-1], refs[-1])

        column = pl.pallas_call(
            order_body,
            out_shape=shape((part_width, model_width), bf16),
            compiler_params=params(),
        )(split_joined[0], split_far)
        split_parts, _ = gather_parts(column, "dp")
        seen_inputs = after(recv_inputs, send_grads)
        seen_grads = after(recv_grads, split_parts[1])
    else:
        recv_grads = exchange(after(send_grads, recv_inputs))
        seen_inputs = after(recv_inputs, send_grads)
        seen_grads = recv_grads

    def forward_body(*refs):
        forward_kernel(rows, *refs)

    kept_inputs, hidden, slope, activation, near_down = pl.pallas_call(
        forward_body,
        in_specs=[anywhere] * 4,
        out_specs=(anywhere,) * 4 + (inside,),
        out_shape=(narrow_out, wide_out, wide_out, wide_out, lying),
        scratch_shapes=[
            narrow, upright, upright, wide, wide, wide, sems(steps), sems(3), sems(4, steps),
        ],
        compiler_params=params(),
    )(seen_inputs, *in_hbm(weight_gate, weight_up, weight_down))

    def delta_body(*refs):
        delta_kernel(rows, *refs)

    both, delta, kept_grads = pl.pallas_call(
        delta_body,
        in_specs=[anywhere] * 5 + [inside],
        out_specs=(inside, anywhere, anywhere),
        out_shape=(
            pltpu.VMEM((slot_count, 2 * hidden_width), bf16),
            narrow_out,
            narrow_out,
        ),
        scratch_shapes=[
            narrow, wide, wide, upright, upright, narrow,
            sems(3, steps), sems(2), sems(2, steps),
        ],
        compiler_params=params(),
    )(*in_hbm(seen_grads), *in_hbm(slope, activation, weight_gate, weight_up), *in_vmem(near_down))
    returned = exchange(delta)

    half = group // 2
    gate_rows, down_rows = sub_width // group, hidden_width // group

    def weight_body(*refs):
        weight_kernel(group, *refs)

    grad_shapes = ((half, gate_rows, 2 * hidden_width), (half, down_rows, sub_width))
    keep_a, keep_b, send_a, send_b = pl.pallas_call(
        weight_body,
        in_specs=[anywhere, anywhere, inside, anywhere],
        out_shape=tuple(shape(dims, f32) for dims in grad_shapes)
        + tuple(shape(dims, bf16) for dims in grad_shapes),
        scratch_shapes=[
            narrow,
            narrow,
            wide,
            pltpu.VMEM((sub_width, 2 * hidden_width), f32),
            pltpu.VMEM((hidden_width, sub_width), f32),
            pltpu.SemaphoreType.DMA((3,)),
        ],
        compiler_params=params(),
        cost_estimate=cost(6 * slot_count * sub_width * hidden_width, 8 * slot_count * hidden_width),
    )(*in_hbm(kept_inputs, kept_grads), *in_vmem(both), *in_hbm(hidden))
    offset = 1
    while 2 * offset < group:
        half //= 2
        got_a, got_b = swap(send_a, "dp", offset), swap(send_b, "dp", offset)
        if in_blocks and offset == 1:
            got_b = after(got_b, split_parts[1])
        keep_a, keep_b, send_a, send_b = pl.pallas_call(
            halve_kernel,
            out_shape=(
                shape((half, gate_rows, 2 * hidden_width), f32),
                shape((half, down_rows, sub_width), f32),
                shape((half, gate_rows, 2 * hidden_width), bf16),
                shape((half, down_rows, sub_width), bf16),
            ),
            compiler_params=params(),
        )(keep_a, keep_b, got_a, got_b)
        offset *= 2
    if in_blocks:
        def interleave_body(*refs):
            interleave_kernel(dp_offsets, block_rows, refs[:-1], refs[-1])

        whole_split = pl.pallas_call(
            interleave_body,
            out_shape=pltpu.VMEM((model_width, model_width), bf16),
            compiler_params=params(),
        )(*split_parts)
        (whole_split,) = in_vmem(whole_split)
    d_tokens = pl.pallas_call(
        split_kernel,
        in_specs=[inside, anywhere, inside],
        out_shape=shape((row_count, model_width), bf16),
        scratch_shapes=[
            narrow,
            pltpu.VMEM((row_count, model_width), bf16),
            pltpu.SemaphoreType.DMA((1,)),
        ],
        compiler_params=params(),
    )(down, returned, whole_split).reshape(batch_count, tok_count, model_width)
    got_a, got_b = swap(send_a, "dp", offset), swap(send_b, "dp", offset)
    got_b = after(got_b, d_tokens)
    shared_gate, shared_up, shared_down = pl.pallas_call(
        last_kernel,
        out_shape=(
            shape((1, gate_rows, hidden_width), f32),
            shape((1, gate_rows, hidden_width), f32),
            shape((1, down_rows, sub_width), f32),
        ),
        compiler_params=params(),
    )(keep_a, keep_b, got_a, got_b)

    return (d_tokens, shared_gate, shared_up, shared_down)


def solution(mesh):
    placed = (
        P(None, ("expert", "dp"), None),
        P(None, ("expert", "dp"), None),
        P(None, ("expert", "dp"), None, None),
        P(None, ("expert", "dp"), None),
        P("expert", None),
        P("expert", None),
        P("expert", None, None),
        P("expert", None, None),
        P("expert", None, None),
    )
    return jax.shard_map(
        on_device,
        mesh=mesh,
        in_specs=placed,
        out_specs=(
            P(None, ("expert", "dp"), None),
            P("expert", "dp", None),
            P("expert", "dp", None),
            P("expert", "dp", None),
        ),
        check_vma=False,
    )
```
